512 devices in a mesh: dp: 4 (over x), fsdp: 128 (over y, z, core).
Axes of the slice: x: 4, y: 4, z: 16, core: 2. Of those that a mesh axis runs over, the one named last changes fastest.
Arguments:
- grads: bfloat16 [4, 64, 2048, 768], P('dp', None, 'fsdp'), may hold values from -400 to 400, as said below
- owners: int32 [64], replicated, may hold values from 0 to 126, as said below
Outputs:
- updates: bfloat16 [64, 2048, 768], P('dp', 'fsdp')
- owner_rms: float32 [4, 128], P('dp', 'fsdp')
The draws below stay inside these ranges and needn't reach their ends.
Inputs may be any that keep to these rules, and one draw needn't show every extreme that they name: Matrix m is updated by replica m // 16; every owner is even; within each aligned block of 16 matrices the owners are distinct. `grads`: gradients are finite reals.
All inputs are finite; a program needn't handle non-finite values.
Results may differ from the reference program's by a relative error of at most 0.015.
Values may be sent and summed in bfloat16 or wider, within the bound.
No kernel may reach another device: no remote copies, remote signals or barrier semaphores. Data moves between devices by JAX's collectives and lax.ppermute only.
A program may use at most 128 MiB of HBM per device.

```python
import math
import jax
import jax.numpy as jnp
from jax import lax

D = 2048
FFE = 768
ITERS = 2
REPLICAS = 4
MATS_DP = 16
MATS = 64
N_FSDP = 128


def draw_grads(key, part):
    key = jax.random.fold_in(key, 11)
    key_rows, key_cols, key_base = jax.random.split(key, 3)
    shape = (REPLICAS, MATS, D, FFE)
    rise = jnp.power(3.0, jnp.arange(D, dtype=jnp.float32) / D)
    rows = jnp.exp(jax.random.uniform(key_rows, (REPLICAS, MATS, D, 1)) * math.log(10.0)) * rise[None, None, :, None]
    cols = jnp.exp(jax.random.uniform(key_cols, (1, MATS, 1, FFE)) * math.log(10.0))
    base = jnp.clip(jax.random.normal(key_base, shape), -6.0, 6.0)
    return (0.1 * base * rows * cols).astype(jnp.bfloat16)


def draw_owners(key, part):
    key = jax.random.fold_in(key, 23)
    key_blocks, key_first, key_shift = jax.random.split(key, 3)
    keys = jax.random.split(key_blocks, REPLICAS)
    pairs = N_FSDP // 2
    top_block = jax.random.randint(key_first, (), 0, REPLICAS).astype(jnp.int32)
    low_block = ((top_block + jax.random.randint(key_shift, (), 1, REPLICAS)) % REPLICAS).astype(jnp.int32)

    def one_block(block_key, block):
        key_perm, key_order = jax.random.split(block_key)
        perm = jax.random.permutation(key_perm, pairs).astype(jnp.int32)
        target = jnp.where(block == top_block, pairs - 1, jnp.where(block == low_block, 0, perm[0])).astype(jnp.int32)
        place = jnp.argmax(perm == target).astype(jnp.int32)
        perm = perm.at[place].set(perm[0]).at[0].set(target)
        order = jax.random.permutation(key_order, MATS_DP)
        return 2 * perm[:MATS_DP][order]
    blocks = jax.vmap(one_block)(keys, jnp.arange(REPLICAS, dtype=jnp.int32))
    return blocks.reshape(MATS).astype(jnp.int32)


def setup_inputs(seed: int = 0) -> dict:
    arg_keys = jax.random.split(jax.random.key(seed), 3)
    grads = draw_grads(jax.random.fold_in(arg_keys[2], 71), 0)
    owners = draw_owners(jax.random.fold_in(arg_keys[2], 71), 0)
    return dict(grads=grads, owners=owners)


COEF_A = 3.4445
COEF_B = -4.775
COEF_C = 2.0315
EPS = 1e-07

def newton(stack):
    summed = lax.optimization_barrier(jnp.sum(stack.astype(jnp.float32), axis=0)).astype(jnp.bfloat16)
    wide = summed.astype(jnp.float32)
    norm = jnp.sqrt(jnp.sum(wide * wide))
    current = (wide / (norm + EPS)).astype(jnp.bfloat16)
    result = None
    for step in range(ITERS):
        gram = jnp.dot(current.T, current, preferred_element_type=jnp.float32).astype(jnp.bfloat16)
        square = jnp.dot(gram, gram, preferred_element_type=jnp.float32)
        poly = (COEF_B * gram.astype(jnp.float32) + COEF_C * square).astype(jnp.bfloat16)
        nxt = COEF_A * current.astype(jnp.float32) + jnp.dot(current, poly, preferred_element_type=jnp.float32)
        if step + 1 < ITERS:
            current = nxt.astype(jnp.bfloat16)
        else:
            result = (math.sqrt(D) * nxt).astype(jnp.bfloat16)
    return (result, norm / math.sqrt(D * FFE))

def reference(grads, owners):
    updates, rms = lax.map(newton, jnp.swapaxes(grads, 0, 1))
    table = owners.reshape(REPLICAS, MATS_DP)
    peers = jnp.arange(N_FSDP, dtype=jnp.int32)
    leads = peers - peers % 2
    hits = (table[:, :, None] == leads[None, None, :]).astype(jnp.float32)
    owner_rms = lax.optimization_barrier(jnp.sum(hits * rms.reshape(REPLICAS, MATS_DP)[:, :, None], axis=1))
    return (updates, owner_rms)
```

```python
import functools
import math

import jax
import jax.numpy as jnp
from jax import lax
from jax.experimental import pallas as pl
from jax.experimental.pallas import tpu as pltpu
from jax.sharding import Mesh
from jax.sharding import PartitionSpec as P

COEF_A = 3.4445
COEF_B = -4.775
COEF_C = 2.0315
EPS = 1e-07

BF16 = jnp.bfloat16
F32 = jnp.float32
VMEM = pl.BlockSpec(memory_space=pltpu.VMEM)
TILE = 256


def columns(i):
    return pl.ds(pl.multiple_of(i * TILE, TILE), TILE)


def dot(a, b):
    return jnp.dot(a, b, preferred_element_type=F32)


def gram_kernel(*refs):
    *pieces, wide_ref, sent_ref, stack = refs
    rows = pieces[0].shape[0]
    for i, piece in enumerate(pieces):
        stack[i * rows : (i + 1) * rows, :] = piece[...]

    @pl.loop(0, wide_ref.shape[1] // TILE)
    def _(n):
        part = lax.dot_general(
            stack[...], stack[:, columns(n)], (((0,), (0,)), ((), ())), preferred_element_type=F32
        )
        wide_ref[:, columns(n)] = part
        sent_ref[:, columns(n)] = part.astype(BF16)


def gram(pieces):
    rows, width = pieces[0].shape
    return pl.pallas_call(
        gram_kernel,
        out_shape=(
            jax.ShapeDtypeStruct((width, width), F32),
            jax.ShapeDtypeStruct((width, width), BF16),
        ),
        in_specs=[VMEM] * len(pieces),
        out_specs=(VMEM, VMEM),
        scratch_shapes=[pltpu.VMEM((rows * len(pieces), width), BF16)],
        compiler_params=pltpu.CompilerParams(vmem_limit_bytes=32 * 2**20),
        cost_estimate=pl.CostEstimate(
            flops=2 * rows * len(pieces) * width * width,
            bytes_accessed=rows * len(pieces) * width * 2 + width * width * 6,
            transcendentals=0,
        ),
    )(*pieces)


def polynomial_kernel(scale, halves, *refs):
    own_ref, other_ref = refs[:2]
    x_refs = refs[2 : 2 + halves]
    u_refs = refs[2 + halves : 2 + 2 * halves]
    norm_ref = refs[2 + 2 * halves]
    g, p, s, s_wide, g1, q = refs[3 + 2 * halves :]
    width = g.shape[0]
    steps = width // TILE

    total = jnp.zeros((), F32)
    for n in range(steps):
        sl = slice(n * TILE, (n + 1) * TILE)
        d = own_ref[sl, sl] + other_ref[sl, sl].astype(F32)
        r = lax.broadcasted_iota(jnp.int32, d.shape, 0)
        c = lax.broadcasted_iota(jnp.int32, d.shape, 1)
        total = total + jnp.sum(jnp.where(r == c, d, 0.0))
    norm = jnp.sqrt(jnp.full(norm_ref.shape, total, F32))
    norm_ref[...] = norm
    inv = 1.0 / (norm + EPS)
    inv = inv[:1, :1]

    @pl.loop(0, steps)
    def _(n):
        sl = columns(n)
        g[:, sl] = ((own_ref[:, sl] + other_ref[:, sl].astype(F32)) * (inv * inv)).astype(BF16)

    @pl.loop(0, steps)
    def _(n):
        sl = columns(n)
        col = g[:, sl]
        p[:, sl] = (COEF_B * col.astype(F32) + COEF_C * dot(g[...], col)).astype(BF16)

    @pl.loop(0, steps)
    def _(n):
        sl = columns(n)
        part = dot(g[...], p[:, sl])
        s[:, sl] = part.astype(BF16)
        s_wide[:, sl] = (2 * COEF_A) * part + (COEF_A * COEF_A) * g[:, sl].astype(F32)

    @pl.loop(0, steps)
    def _(n):
        sl = columns(n)
        g1[:, sl] = (s_wide[:, sl] + dot(p[...], s[:, sl])).astype(BF16)

    @pl.loop(0, steps)
    def _(n):
        sl = columns(n)
        col = g1[:, sl]
        q[:, sl] = (COEF_B * col.astype(F32) + COEF_C * dot(g1[...], col)).astype(BF16)

    for x_ref, u_ref in zip(x_refs, u_refs):
        x = x_ref[...]
        x1 = (inv * (COEF_A * x.astype(F32) + dot(x, p[...]))).astype(BF16)
        u_ref[...] = (scale * (COEF_A * x1.astype(F32) + dot(x1, q[...]))).astype(BF16)


def polynomial(own, other, xs, full_rows):
    width = own.shape[0]
    rows = sum(x.shape[0] for x in xs)
    mat = pltpu.VMEM((width, width), BF16)
    *updates, norm = pl.pallas_call(
        functools.partial(polynomial_kernel, math.sqrt(full_rows), len(xs)),
        out_shape=tuple(jax.ShapeDtypeStruct(x.shape, BF16) for x in xs)
        + (jax.ShapeDtypeStruct((8, 128), F32),),
        in_specs=[VMEM] * (2 + len(xs)),
        out_specs=(VMEM,) * (1 + len(xs)),
        scratch_shapes=[mat, mat, mat, pltpu.VMEM((width, width), F32), mat, mat],
        compiler_params=pltpu.CompilerParams(vmem_limit_bytes=32 * 2**20),
        cost_estimate=pl.CostEstimate(
            flops=8 * width**3 + 4 * rows * width * width,
            bytes_accessed=width * width * 6 + rows * width * 4,
            transcendentals=0,
        ),
    )(own, other, *xs)
    return updates, norm


def shift(value, axis, distance):
    n = lax.axis_size(axis)
    return lax.ppermute(value, axis, [(i, (i + distance) % n) for i in range(n)])


def on_device(grads, owners):
    block = grads[0]
    mats, rows_dev, width = block.shape
    dp_n = lax.axis_size("dp")
    y_n, z_n, core_n = lax.axis_size("y"), lax.axis_size("z"), lax.axis_size("core")
    mats_dp = mats // dp_n
    full_rows = y_n * z_n * core_n * rows_dev
    halves = 2
    part = rows_dev // halves

    own, pieces = [], []
    for h in range(halves):
        slabs = block[:, h * part : (h + 1) * part, :].reshape(dp_n, mats_dp, part, width)
        replicas = lax.all_to_all(slabs, "dp", 0, 0, tiled=True)
        summed = jnp.sum(replicas.astype(F32), axis=0).astype(BF16)
        mine = lax.all_to_all(summed, "z", 0, 0, tiled=True).reshape(z_n * part, width)
        own.append(mine)
        pieces += [mine] + [shift(mine, "y", k) for k in range(1, y_n)]

    gram_wide, gram_sent = gram(pieces)
    gram_other = shift(gram_sent, "core", 1)
    updates, norm = polynomial(gram_wide, gram_other, own, full_rows)

    lanes = 128
    tiles = width // lanes
    slab = jnp.stack([u.reshape(z_n, part, tiles, lanes) for u in updates], axis=1)
    slab = slab.transpose(0, 1, 3, 2, 4).reshape(z_n, rows_dev * tiles, lanes)
    high = norm.astype(BF16)
    low = (norm - high.astype(F32)).astype(BF16)
    note = jnp.concatenate([high[:4], low[:4]], axis=0)
    slab = jnp.concatenate([slab, jnp.broadcast_to(note, (z_n, 8, lanes))], axis=1)
    back = lax.all_to_all(slab, "z", 0, 0, tiled=True)
    out = back[:, : rows_dev * tiles].reshape(z_n, halves, tiles, part, lanes)
    out = out.transpose(0, 1, 3, 2, 4).reshape(z_n, rows_dev, width)
    norms = (back[:, rows_dev * tiles, 0].astype(F32) + back[:, rows_dev * tiles + 4, 0].astype(F32))

    index = (lax.axis_index("y") * z_n + lax.axis_index("z")) * core_n + lax.axis_index("core")
    mine = lax.dynamic_slice_in_dim(owners, lax.axis_index("dp") * mats_dp, mats_dp)
    hits = mine == index - index % core_n
    owner_rms = jnp.sum(jnp.where(hits, norms, 0.0)) / math.sqrt(full_rows * width)
    return out, owner_rms.reshape(1, 1)


def solution(mesh):
    dp_n, fsdp_n = mesh.devices.shape
    grid = Mesh(mesh.devices.reshape(dp_n, 4, fsdp_n // 8, 2), ("dp", "y", "z", "core"))
    fsdp = ("y", "z", "core")
    in_specs = (P("dp", None, fsdp, None), P())
    out_specs = (P("dp", fsdp, None), P("dp", fsdp))
    return jax.shard_map(
        on_device, mesh=grid, in_specs=in_specs, out_specs=out_specs, check_vma=False
    )
```

```python
import functools
import math

import jax
import jax.numpy as jnp
from jax import lax
from jax.experimental import pallas as pl
from jax.experimental.pallas import tpu as pltpu
from jax.sharding import Mesh
from jax.sharding import PartitionSpec as P

COEF_A = 3.4445
COEF_B = -4.775
COEF_C = 2.0315
EPS = 1e-07

BF16 = jnp.bfloat16
F32 = jnp.float32
VMEM = pl.BlockSpec(memory_space=pltpu.VMEM)
SMEM = pl.BlockSpec(memory_space=pltpu.SMEM)
TILE = 256
LANES = 128
NOTE = 8


def dot(a, b):
    return jnp.dot(a, b, preferred_element_type=F32)


def gram_of(a, b):
    return lax.dot_general(a, b, (((0,), (0,)), ((), ())), preferred_element_type=F32)


def lower(width):
    return [(slice(j, width), slice(j, j + TILE)) for j in range(0, width, TILE)]


def store_symmetric(ref, rows, cols, value):
    ref[rows, cols] = value
    if cols.stop < rows.stop:
        ref[cols, cols.stop : rows.stop] = value[TILE:].T


def gram_kernel(*refs):
    *pieces, total_ref, stack = refs
    rows = pieces[0].shape[0]
    for i, piece in enumerate(pieces):
        stack[i * rows : (i + 1) * rows, :] = piece[...]
    for down, cols in lower(total_ref.shape[0]):
        total_ref[down, cols] = gram_of(stack[:, down], stack[:, cols])


def gram(pieces):
    rows, width = pieces[0].shape
    return pl.pallas_call(
        gram_kernel,
        out_shape=jax.ShapeDtypeStruct((width, width), F32),
        in_specs=[VMEM] * len(pieces),
        out_specs=VMEM,
        scratch_shapes=[pltpu.VMEM((rows * len(pieces), width), BF16)],
        compiler_params=pltpu.CompilerParams(vmem_limit_bytes=32 * 2**20),
        cost_estimate=pl.CostEstimate(
            flops=2 * rows * len(pieces) * width * width,
            bytes_accessed=rows * len(pieces) * width * 2 + width * width * 4,
            transcendentals=0,
        ),
    )(*pieces)


def polynomial_kernel(scale, count, *refs):
    total_ref, x_ref = refs[:2]
    pieces = refs[2 : 2 + count]
    slab_ref = refs[2 + count]
    stack, wide, g, p, s = refs[3 + count :]
    width = g.shape[0]
    rows = pieces[0].shape[0]

    for i, piece in enumerate(pieces):
        stack[i * rows : (i + 1) * rows, :] = piece[...]
    trace = jnp.zeros((1, 1), F32)
    for down, cols in lower(width):
        part = total_ref[down, cols] + gram_of(stack[:, down], stack[:, cols])
        wide[down, cols] = part
        d = part[:TILE]
        r = lax.broadcasted_iota(jnp.int32, d.shape, 0)
        c = lax.broadcasted_iota(jnp.int32, d.shape, 1)
        trace = trace + jnp.sum(jnp.where(r == c, d, 0.0), keepdims=True)
    norm = jnp.sqrt(trace)
    inv = 1.0 / (norm + EPS)

    for down, cols in lower(width):
        store_symmetric(g, down, cols, (wide[down, cols] * (inv * inv)).astype(BF16))
    for down, cols in lower(width):
        part = COEF_B * g[down, cols].astype(F32) + COEF_C * dot(g[down, :], g[:, cols])
        store_symmetric(p, down, cols, part.astype(BF16))
    for down, cols in lower(width):
        part = dot(g[down, :], p[:, cols])
        wide[down, cols] = (2 * COEF_A) * part + (COEF_A * COEF_A) * g[down, cols].astype(F32)
        store_symmetric(s, down, cols, part.astype(BF16))
    for down, cols in lower(width):
        part = wide[down, cols] + dot(p[down, :], s[:, cols])
        store_symmetric(g, down, cols, part.astype(BF16))
    for down, cols in lower(width):
        part = COEF_B * g[down, cols].astype(F32) + COEF_C * dot(g[down, :], g[:, cols])
        store_symmetric(s, down, cols, part.astype(BF16))

    x = x_ref[...]
    x1 = (inv * (COEF_A * x.astype(F32) + dot(x, p[...]))).astype(BF16)
    update = (scale * (COEF_A * x1.astype(F32) + dot(x1, s[...]))).astype(BF16)
    blocks, high, _ = slab_ref.shape
    tall = update.shape[0] // blocks
    for i in range(width // LANES):
        slab_ref[:, i * tall : (i + 1) * tall, :] = update[:, i * LANES : (i + 1) * LANES].reshape(
            blocks, tall, LANES
        )
    first = norm.astype(BF16).astype(F32)
    second = norm - first
    note = lax.broadcasted_iota(jnp.int32, (NOTE, LANES), 0)
    note = jnp.where(note < NOTE // 2, first, second).astype(BF16)
    slab_ref[:, high - NOTE :, :] = jnp.broadcast_to(note, (blocks, NOTE, LANES))


def polynomial(total, x, pieces, full_rows, blocks):
    width = total.shape[0]
    rows = x.shape[0]
    mat = pltpu.VMEM((width, width), BF16)
    high = rows // blocks * width // LANES + NOTE
    return pl.pallas_call(
        functools.partial(polynomial_kernel, math.sqrt(full_rows), len(pieces)),
        out_shape=jax.ShapeDtypeStruct((blocks, high, LANES), BF16),
        in_specs=[VMEM] * (2 + len(pieces)),
        out_specs=VMEM,
        scratch_shapes=[
            pltpu.VMEM((len(pieces) * pieces[0].shape[0], width), BF16),
            pltpu.VMEM((width, width), F32),
            mat,
            mat,
            mat,
        ],
        compiler_params=pltpu.CompilerParams(vmem_limit_bytes=32 * 2**20),
        cost_estimate=pl.CostEstimate(
            flops=6 * width**3 + 6 * rows * width * width,
            bytes_accessed=width * width * 4 + rows * width * 8,
            transcendentals=0,
        ),
    )(total, x, *pieces)


def place_kernel(count, back_ref, hit_ref, out_ref, rms_ref):
    blocks, tall, width = out_ref.shape
    for i in range(width // LANES):
        out_ref[:, :, i * LANES : (i + 1) * LANES] = back_ref[:, i * tall : (i + 1) * tall, :]
    note = back_ref[:, back_ref.shape[1] - NOTE :, :].astype(F32)
    norms = note[:, :1, :1] + note[:, NOTE // 2 : NOTE // 2 + 1, :1]
    rms_ref[0, 0] = jnp.sum(jnp.where(hit_ref[...] > 0, norms, 0.0)) / math.sqrt(count)


def place(back, hits, tall, width, full_rows):
    blocks = back.shape[0]
    return pl.pallas_call(
        functools.partial(place_kernel, full_rows * width),
        out_shape=(
            jax.ShapeDtypeStruct((blocks, tall, width), BF16),
            jax.ShapeDtypeStruct((1, 1), F32),
        ),
        in_specs=[VMEM, VMEM],
        out_specs=(VMEM, SMEM),
    )(back, hits.astype(jnp.int32).reshape(blocks, 1, 1))


def shift(value, axis, distance):
    n = lax.axis_size(axis)
    return lax.ppermute(value, axis, [(i, (i + distance) % n) for i in range(n)])


def on_device(grads, owners):
    block = grads[0]
    mats, rows_dev, width = block.shape
    dp_n = lax.axis_size("dp")
    y_n, z_n, core_n = lax.axis_size("y"), lax.axis_size("z"), lax.axis_size("core")
    mats_dp = mats // dp_n
    full_rows = y_n * z_n * core_n * rows_dev

    slabs = block.reshape(dp_n, mats_dp, rows_dev, width)
    replicas = lax.all_to_all(slabs, "dp", 0, 0, tiled=True)
    summed = jnp.sum(replicas.astype(F32), axis=0).astype(BF16)
    mine = lax.all_to_all(summed, "z", 0, 0, tiled=True).reshape(z_n * rows_dev, width)

    far = shift(mine, "y", 2)
    near = [mine, shift(mine, "y", 1), shift(mine, "y", 3)]
    near += [shift(piece, "core", 1) for piece in near]
    far = [far, shift(far, "core", 1)]
    slab = polynomial(gram(near), mine, far, full_rows, z_n)
    back = lax.all_to_all(slab, "z", 0, 0, tiled=True)

    index = (lax.axis_index("y") * z_n + lax.axis_index("z")) * core_n + lax.axis_index("core")
    owned = lax.dynamic_slice_in_dim(owners, lax.axis_index("dp") * mats_dp, mats_dp)
    hits = owned == index - index % core_n
    return place(back, hits, rows_dev, width, full_rows)


def solution(mesh):
    dp_n, fsdp_n = mesh.devices.shape
    grid = Mesh(mesh.devices.reshape(dp_n, 4, fsdp_n // 8, 2), ("dp", "y", "z", "core"))
    fsdp = ("y", "z", "core")
    in_specs = (P("dp", None, fsdp, None), P())
    out_specs = (P("dp", fsdp, None), P("dp", fsdp))
    return jax.shard_map(
        on_device, mesh=grid, in_specs=in_specs, out_specs=out_specs, check_vma=False
    )
```

```python
import functools
import math

import jax
import jax.numpy as jnp
from jax import lax
from jax.experimental import pallas as pl
from jax.experimental.pallas import tpu as pltpu
from jax.sharding import Mesh
from jax.sharding import PartitionSpec as P

COEF_A = 3.4445
COEF_B = -4.775
COEF_C = 2.0315
EPS = 1e-07

BF16 = jnp.bfloat16
F32 = jnp.float32
VMEM = pl.BlockSpec(memory_space=pltpu.VMEM)
SMEM = pl.BlockSpec(memory_space=pltpu.SMEM)
TILE = 256
LANES = 128
NOTE = 8


def dot(a, b):
    return jnp.dot(a, b, preferred_element_type=F32)


def gram_of(a, b):
    return lax.dot_general(a, b, (((0,), (0,)), ((), ())), preferred_element_type=F32)


def lower(width):
    return [(slice(j, width), slice(j, j + TILE)) for j in range(0, width, TILE)]


def store_symmetric(ref, rows, cols, value):
    ref[rows, cols] = value
    if cols.stop < rows.stop:
        ref[cols, cols.stop : rows.stop] = value[TILE:].T


def indices(shape):
    return (lax.broadcasted_iota(jnp.int32, shape, d) for d in range(2))


def diagonal(block):
    row, col = indices(block.shape)
    return jnp.sum(jnp.where(row == col, block, 0.0), axis=0, keepdims=True)


def merge(one, two):
    row, col = indices(one.shape)
    return jnp.where(row >= col, one, two), diagonal(two)


def split(both, second_diagonal):
    row, col = indices(both.shape)
    other = both.T
    two = jnp.where(row < col, both, jnp.where(row == col, second_diagonal, other))
    return jnp.where(row >= col, both, other), two


SMALL = TILE // 2
SPARE = 16
HALF = 2 * TILE + SMALL // 2 + SPARE


def gram_kernel(core_ref, mine_ref, other_ref, wide_ref, sent_ref, stack):
    rows = mine_ref.shape[0]
    stack[:rows, :] = mine_ref[...]
    stack[rows:, :] = other_ref[...]
    first = core_ref[0] == 0
    one, two, three = (stack[:, i * TILE : (i + 1) * TILE] for i in range(3))
    below = gram_of(stack[:, TILE:], one)
    middle = gram_of(stack[:, TILE:], two)
    last = gram_of(three, three)
    corner, corner_diagonal = merge(gram_of(one, one), middle[:TILE])
    tip, tip_diagonal = merge(last[:SMALL, :SMALL], last[SMALL:, SMALL:])

    def store(span, lanes, value):
        wide_ref[span, lanes] = value
        sent_ref[span, lanes] = value.astype(BF16)

    every = slice(0, TILE)
    store(slice(0, TILE), every, jnp.where(first, below[:TILE], middle[TILE:]))
    store(slice(TILE, 2 * TILE), every, jnp.where(first, below[TILE:], corner))
    small = jnp.where(first, tip, last[SMALL:, :SMALL])
    span = slice(2 * TILE, HALF - SPARE)
    store(span, slice(0, SMALL), small[: SMALL // 2])
    store(span, slice(SMALL, TILE), small[SMALL // 2 :])
    span = slice(HALF - SPARE, HALF)
    left, right = corner_diagonal[:, :SMALL], corner_diagonal[:, SMALL:]
    store(span, slice(0, SMALL), jnp.broadcast_to(jnp.where(first, tip_diagonal, left), (SPARE, SMALL)))
    store(span, slice(SMALL, TILE), jnp.broadcast_to(jnp.where(first, 0.0, right), (SPARE, SMALL)))


def half_gram(core, mine, other):
    rows, width = mine.shape
    assert width == 3 * TILE
    shape = (HALF, TILE)
    return pl.pallas_call(
        gram_kernel,
        out_shape=(jax.ShapeDtypeStruct(shape, F32), jax.ShapeDtypeStruct(shape, BF16)),
        in_specs=[SMEM, VMEM, VMEM],
        out_specs=(VMEM, VMEM),
        scratch_shapes=[pltpu.VMEM((2 * rows, width), BF16)],
        compiler_params=pltpu.CompilerParams(vmem_limit_bytes=32 * 2**20),
        cost_estimate=pl.CostEstimate(
            flops=2 * rows * width * width,
            bytes_accessed=rows * width * 4 + shape[0] * TILE * 6,
            transcendentals=0,
        ),
    )(core, mine, other)


def polynomial_kernel(scale, core_ref, own_ref, other_ref, x_ref, slab_ref, wide, g, p, s):
    width = g.shape[0]
    core = core_ref[0]

    def pick(half, span):
        return jnp.where(core == half, own_ref[span, :], other_ref[span, :].astype(F32))

    def place(i, j, value, size=TILE):
        wide[i * size : i * size + value.shape[0], j * size : j * size + value.shape[1]] = value

    def small(half):
        value = pick(half, slice(2 * TILE, HALF - SPARE))
        return jnp.concatenate([value[:, :SMALL], value[:, SMALL:]], axis=0)

    spare = slice(HALF - SPARE, HALF - SPARE + 8)
    tip_diagonal, corner_diagonal = pick(0, spare)[:1, :SMALL], pick(1, spare)[:1]
    corner, tip = pick(1, slice(TILE, 2 * TILE)), small(0)
    place(1, 0, pick(0, slice(0, TILE)))
    place(2, 0, pick(0, slice(TILE, 2 * TILE)))
    place(2, 1, pick(1, slice(0, TILE)))
    one, two = split(corner, corner_diagonal)
    place(0, 0, one)
    place(1, 1, two)
    one, two = split(tip, tip_diagonal)
    bend = small(1)
    place(4, 4, one, SMALL)
    place(5, 5, two, SMALL)
    place(5, 4, bend, SMALL)
    place(4, 5, bend.T, SMALL)
    trace = sum(
        jnp.sum(part, axis=1, keepdims=True)
        for part in (diagonal(corner), corner_diagonal, diagonal(tip), tip_diagonal)
    )
    norm = jnp.sqrt(trace)
    inv = 1.0 / (norm + EPS)

    for down, cols in lower(width):
        store_symmetric(g, down, cols, (wide[down, cols] * (inv * inv)).astype(BF16))
    for down, cols in lower(width):
        part = COEF_B * g[down, cols].astype(F32) + COEF_C * dot(g[down, :], g[:, cols])
        store_symmetric(p, down, cols, part.astype(BF16))
    for down, cols in lower(width):
        part = dot(g[down, :], p[:, cols])
        wide[down, cols] = (2 * COEF_A) * part + (COEF_A * COEF_A) * g[down, cols].astype(F32)
        store_symmetric(s, down, cols, part.astype(BF16))
    for down, cols in lower(width):
        part = wide[down, cols] + dot(p[down, :], s[:, cols])
        store_symmetric(g, down, cols, part.astype(BF16))
    for down, cols in lower(width):
        part = COEF_B * g[down, cols].astype(F32) + COEF_C * dot(g[down, :], g[:, cols])
        store_symmetric(s, down, cols, part.astype(BF16))

    x = x_ref[...]
    x1 = (inv * (COEF_A * x.astype(F32) + dot(x, p[...]))).astype(BF16)
    update = (scale * (COEF_A * x1.astype(F32) + dot(x1, s[...]))).astype(BF16)
    blocks, high, _ = slab_ref.shape
    tall = update.shape[0] // blocks
    for i in range(width // LANES):
        slab_ref[:, i * tall : (i + 1) * tall, :] = update[:, i * LANES : (i + 1) * LANES].reshape(
            blocks, tall, LANES
        )
    first = norm.astype(BF16).astype(F32)
    second = norm - first
    note = lax.broadcasted_iota(jnp.int32, (NOTE, LANES), 0)
    note = jnp.where(note < NOTE // 2, first, second).astype(BF16)
    slab_ref[:, high - NOTE :, :] = jnp.broadcast_to(note, (blocks, NOTE, LANES))


def polynomial(core, own, other, x, full_rows, blocks):
    rows, width = x.shape
    mat = pltpu.VMEM((width, width), BF16)
    high = rows // blocks * width // LANES + NOTE
    return pl.pallas_call(
        functools.partial(polynomial_kernel, math.sqrt(full_rows)),
        out_shape=jax.ShapeDtypeStruct((blocks, high, LANES), BF16),
        in_specs=[SMEM, VMEM, VMEM, VMEM],
        out_specs=VMEM,
        scratch_shapes=[pltpu.VMEM((width, width), F32), mat, mat, mat],
        compiler_params=pltpu.CompilerParams(vmem_limit_bytes=32 * 2**20),
        cost_estimate=pl.CostEstimate(
            flops=6 * width**3 + 4 * rows * width * width,
            bytes_accessed=width * width * 3 + rows * width * 4,
            transcendentals=0,
        ),
    )(core, own, other, x)


def place_kernel(count, back_ref, hit_ref, out_ref, rms_ref):
    tall, width = out_ref.shape[1:]
    for i in range(width // LANES):
        out_ref[:, :, i * LANES : (i + 1) * LANES] = back_ref[:, i * tall : (i + 1) * tall, :]
    note = back_ref[:, back_ref.shape[1] - NOTE :, :].astype(F32)
    norms = note[:, :1, :1] + note[:, NOTE // 2 : NOTE // 2 + 1, :1]
    mine = jnp.sum(jnp.where(hit_ref[...] > 0, norms, 0.0)) / math.sqrt(count)
    step = pl.program_id(0)

    @pl.when(step == 0)
    def _():
        rms_ref[0, 0] = mine

    @pl.when(step > 0)
    def _():
        rms_ref[0, 0] = rms_ref[0, 0] + mine


def place(back, hits, tall, width, full_rows):
    blocks, high, lanes = back.shape
    group = blocks // 2
    return pl.pallas_call(
        functools.partial(place_kernel, full_rows * width),
        grid=(blocks // group,),
        out_shape=(
            jax.ShapeDtypeStruct((blocks, tall, width), BF16),
            jax.ShapeDtypeStruct((1, 1), F32),
        ),
        in_specs=[
            pl.BlockSpec((group, high, lanes), lambda i: (i, 0, 0)),
            pl.BlockSpec((group, 1, 1), lambda i: (i, 0, 0)),
        ],
        out_specs=(pl.BlockSpec((group, tall, width), lambda i: (i, 0, 0)), SMEM),
        compiler_params=pltpu.CompilerParams(vmem_limit_bytes=60 * 2**20),
    )(back, hits.astype(jnp.int32).reshape(blocks, 1, 1))


def shift(value, axis, distance):
    n = lax.axis_size(axis)
    return lax.ppermute(value, axis, [(i, (i + distance) % n) for i in range(n)])


def neighbour(value, axis, turn):
    ring, core_n = lax.axis_size(axis), lax.axis_size("core")
    pairs = []
    for at in range(ring):
        for core in range(core_n):
            other = at ^ 1 if (turn + core) % 2 == 0 else ring - 1 - at
            pairs.append((at * core_n + core, other * core_n + core))
    return lax.ppermute(value, (axis, "core"), pairs)


def on_device(grads, owners):
    block = grads[0]
    mats, rows_dev, width = block.shape
    dp_n = lax.axis_size("dp")
    y_n, core_n = lax.axis_size("y"), lax.axis_size("core")
    zh_n, zl_n = lax.axis_size("zh"), lax.axis_size("zl")
    z_n = y_n * zl_n
    mats_dp = mats // dp_n
    full_rows = zh_n * z_n * core_n * rows_dev

    slabs = block.reshape(dp_n, mats_dp, rows_dev, width)
    replicas = lax.all_to_all(slabs, "dp", 0, 0, tiled=True)
    summed = jnp.sum(replicas.astype(F32), axis=0).astype(BF16)
    mine = lax.all_to_all(summed, ("y", "zl"), 0, 0, tiled=True).reshape(z_n * rows_dev, width)

    core = lax.axis_index("core").astype(jnp.int32).reshape(1)
    total, sent = half_gram(core, mine, shift(mine, "core", 1))
    cut = HALF // 2 // SPARE * SPARE
    totals = [total[:cut], total[cut:]]
    sents = [sent[:cut], sent[cut:]]
    for turn in range(2):
        came = [neighbour(part, "zh", turn + i) for i, part in enumerate(sents)]
        totals = [part + other.astype(F32) for part, other in zip(totals, came)]
        sents = [part.astype(BF16) for part in totals]
    total, sent = jnp.concatenate(totals), jnp.concatenate(sents)
    slab = polynomial(core, total, shift(sent, "core", 1), mine, full_rows, z_n)
    back = lax.all_to_all(slab, ("y", "zl"), 0, 0, tiled=True)

    index = (lax.axis_index("y") * zh_n + lax.axis_index("zh")) * zl_n + lax.axis_index("zl")
    index = index * core_n + lax.axis_index("core")
    owned = lax.dynamic_slice_in_dim(owners, lax.axis_index("dp") * mats_dp, mats_dp)
    hits = owned == index - index % core_n
    return place(back, hits, rows_dev, width, full_rows)


def solution(mesh):
    dp_n, fsdp_n = mesh.devices.shape
    grid = Mesh(mesh.devices.reshape(dp_n, 4, 4, fsdp_n // 32, 2), ("dp", "y", "zh", "zl", "core"))
    fsdp = ("y", "zh", "zl", "core")
    in_specs = (P("dp", None, fsdp, None), P())
    out_specs = (P("dp", fsdp, None), P("dp", fsdp))
    return jax.shard_map(
        on_device, mesh=grid, in_specs=in_specs, out_specs=out_specs, check_vma=False
    )
```

```python
import functools
import math

import jax
import jax.numpy as jnp
from jax import lax
from jax.experimental import pallas as pl
from jax.experimental.pallas import tpu as pltpu
from jax.sharding import Mesh
from jax.sharding import PartitionSpec as P

COEF_A = 3.4445
COEF_B = -4.775
COEF_C = 2.0315
EPS = 1e-07

BF16 = jnp.bfloat16
F32 = jnp.float32
VMEM = pl.BlockSpec(memory_space=pltpu.VMEM)
SMEM = pl.BlockSpec(memory_space=pltpu.SMEM)
TILE = 256
FSDP = ("y", "zh", "zm", "zb", "core")
LANES = 128
NOTE = 8


def dot(a, b):
    return jnp.dot(a, b, preferred_element_type=F32)


def gram_of(a, b):
    return lax.dot_general(a, b, (((0,), (0,)), ((), ())), preferred_element_type=F32)


def lower(width):
    return [(slice(j, width), slice(j, j + TILE)) for j in range(0, width, TILE)]


def store_symmetric(ref, rows, cols, value):
    ref[rows, cols] = value
    if cols.stop < rows.stop:
        ref[cols, cols.stop : rows.stop] = value[TILE:].T


def indices(shape):
    return (lax.broadcasted_iota(jnp.int32, shape, d) for d in range(2))


def diagonal(block):
    row, col = indices(block.shape)
    return jnp.sum(jnp.where(row == col, block, 0.0), axis=0, keepdims=True)


def merge(one, two):
    row, col = indices(one.shape)
    return jnp.where(row >= col, one, two), diagonal(two)


def split(both, second_diagonal):
    row, col = indices(both.shape)
    other = both.T
    two = jnp.where(row < col, both, jnp.where(row == col, second_diagonal, other))
    return jnp.where(row >= col, both, other), two


SMALL = TILE // 2
SPARE = 16
HALF = 2 * TILE + SMALL // 2 + SPARE


def gram_kernel(core_ref, *refs):
    *pieces, wide_ref, sent_ref, stack = refs
    rows = pieces[0].shape[0]
    for i, piece in enumerate(pieces):
        stack[i * rows : (i + 1) * rows, :] = piece[...]
    first = core_ref[0] == 0
    one, two, three = (stack[:, i * TILE : (i + 1) * TILE] for i in range(3))
    below = gram_of(stack[:, TILE:], one)
    middle = gram_of(stack[:, TILE:], two)
    last = gram_of(three, three)
    corner, corner_diagonal = merge(gram_of(one, one), middle[:TILE])
    tip, tip_diagonal = merge(last[:SMALL, :SMALL], last[SMALL:, SMALL:])

    def store(span, lanes, value):
        wide_ref[span, lanes] = value
        sent_ref[span, lanes] = value.astype(BF16)

    every = slice(0, TILE)
    store(slice(0, TILE), every, jnp.where(first, below[:TILE], middle[TILE:]))
    store(slice(TILE, 2 * TILE), every, jnp.where(first, below[TILE:], corner))
    small = jnp.where(first, tip, last[SMALL:, :SMALL])
    span = slice(2 * TILE, HALF - SPARE)
    store(span, slice(0, SMALL), small[: SMALL // 2])
    store(span, slice(SMALL, TILE), small[SMALL // 2 :])
    span = slice(HALF - SPARE, HALF)
    left, right = corner_diagonal[:, :SMALL], corner_diagonal[:, SMALL:]
    store(span, slice(0, SMALL), jnp.broadcast_to(jnp.where(first, tip_diagonal, left), (SPARE, SMALL)))
    store(span, slice(SMALL, TILE), jnp.broadcast_to(jnp.where(first, 0.0, right), (SPARE, SMALL)))


def half_gram(core, pieces):
    rows, width = pieces[0].shape
    assert width == 3 * TILE
    shape = (HALF, TILE)
    return pl.pallas_call(
        gram_kernel,
        out_shape=(jax.ShapeDtypeStruct(shape, F32), jax.ShapeDtypeStruct(shape, BF16)),
        in_specs=[SMEM] + [VMEM] * len(pieces),
        out_specs=(VMEM, VMEM),
        scratch_shapes=[pltpu.VMEM((len(pieces) * rows, width), BF16)],
        compiler_params=pltpu.CompilerParams(vmem_limit_bytes=32 * 2**20),
        cost_estimate=pl.CostEstimate(
            flops=len(pieces) * rows * width * width,
            bytes_accessed=len(pieces) * rows * width * 2 + shape[0] * TILE * 6,
            transcendentals=0,
        ),
    )(core, *pieces)


def polynomial_kernel(scale, core_ref, own_ref, other_ref, x_ref, slab_ref, wide, g, p, s):
    width = g.shape[0]
    core = core_ref[0]

    def pick(half, span):
        return jnp.where(core == half, own_ref[span, :], other_ref[span, :].astype(F32))

    def place(i, j, value, size=TILE):
        wide[i * size : i * size + value.shape[0], j * size : j * size + value.shape[1]] = value

    def small(half):
        value = pick(half, slice(2 * TILE, HALF - SPARE))
        return jnp.concatenate([value[:, :SMALL], value[:, SMALL:]], axis=0)

    spare = slice(HALF - SPARE, HALF - SPARE + 8)
    tip_diagonal, corner_diagonal = pick(0, spare)[:1, :SMALL], pick(1, spare)[:1]
    corner, tip = pick(1, slice(TILE, 2 * TILE)), small(0)
    place(1, 0, pick(0, slice(0, TILE)))
    place(2, 0, pick(0, slice(TILE, 2 * TILE)))
    place(2, 1, pick(1, slice(0, TILE)))
    one, two = split(corner, corner_diagonal)
    place(0, 0, one)
    place(1, 1, two)
    one, two = split(tip, tip_diagonal)
    bend = small(1)
    place(4, 4, one, SMALL)
    place(5, 5, two, SMALL)
    place(5, 4, bend, SMALL)
    place(4, 5, bend.T, SMALL)
    trace = sum(
        jnp.sum(part, axis=1, keepdims=True)
        for part in (diagonal(corner), corner_diagonal, diagonal(tip), tip_diagonal)
    )
    norm = jnp.sqrt(trace)
    inv = 1.0 / (norm + EPS)

    for down, cols in lower(width):
        store_symmetric(g, down, cols, (wide[down, cols] * (inv * inv)).astype(BF16))
    for down, cols in lower(width):
        part = COEF_B * g[down, cols].astype(F32) + COEF_C * dot(g[down, :], g[:, cols])
        store_symmetric(p, down, cols, part.astype(BF16))
    for down, cols in lower(width):
        part = dot(g[down, :], p[:, cols])
        wide[down, cols] = (2 * COEF_A) * part + (COEF_A * COEF_A) * g[down, cols].astype(F32)
        store_symmetric(s, down, cols, part.astype(BF16))
    for down, cols in lower(width):
        part = wide[down, cols] + dot(p[down, :], s[:, cols])
        store_symmetric(g, down, cols, part.astype(BF16))
    for down, cols in lower(width):
        part = COEF_B * g[down, cols].astype(F32) + COEF_C * dot(g[down, :], g[:, cols])
        store_symmetric(s, down, cols, part.astype(BF16))

    x = x_ref[...]
    x1 = (inv * (COEF_A * x.astype(F32) + dot(x, p[...]))).astype(BF16)
    update = (scale * (COEF_A * x1.astype(F32) + dot(x1, s[...]))).astype(BF16)
    blocks, high, _ = slab_ref.shape
    tall = update.shape[0] // blocks
    for i in range(width // LANES):
        slab_ref[:, i * tall : (i + 1) * tall, :] = update[:, i * LANES : (i + 1) * LANES].reshape(
            blocks, tall, LANES
        )
    first = norm.astype(BF16).astype(F32)
    second = norm - first
    note = lax.broadcasted_iota(jnp.int32, (NOTE, LANES), 0)
    note = jnp.where(note < NOTE // 2, first, second).astype(BF16)
    slab_ref[:, high - NOTE :, :] = jnp.broadcast_to(note, (blocks, NOTE, LANES))


def polynomial(core, own, other, x, full_rows, blocks):
    rows, width = x.shape
    mat = pltpu.VMEM((width, width), BF16)
    high = rows // blocks * width // LANES + NOTE
    return pl.pallas_call(
        functools.partial(polynomial_kernel, math.sqrt(full_rows)),
        out_shape=jax.ShapeDtypeStruct((blocks, high, LANES), BF16),
        in_specs=[SMEM, VMEM, VMEM, VMEM],
        out_specs=VMEM,
        scratch_shapes=[pltpu.VMEM((width, width), F32), mat, mat, mat],
        compiler_params=pltpu.CompilerParams(vmem_limit_bytes=32 * 2**20),
        cost_estimate=pl.CostEstimate(
            flops=6 * width**3 + 4 * rows * width * width,
            bytes_accessed=width * width * 3 + rows * width * 4,
            transcendentals=0,
        ),
    )(core, own, other, x)


def place_kernel(count, back_ref, hit_ref, out_ref, rms_ref):
    tall, width = out_ref.shape[1:]
    for i in range(width // LANES):
        out_ref[:, :, i * LANES : (i + 1) * LANES] = back_ref[:, i * tall : (i + 1) * tall, :]
    note = back_ref[:, back_ref.shape[1] - NOTE :, :].astype(F32)
    norms = note[:, :1, :1] + note[:, NOTE // 2 : NOTE // 2 + 1, :1]
    mine = jnp.sum(jnp.where(hit_ref[...] > 0, norms, 0.0)) / math.sqrt(count)
    step = pl.program_id(0)

    @pl.when(step == 0)
    def _():
        rms_ref[0, 0] = mine

    @pl.when(step > 0)
    def _():
        rms_ref[0, 0] = rms_ref[0, 0] + mine


def place(back, hits, tall, width, full_rows):
    blocks, high, lanes = back.shape
    group = blocks // 2
    return pl.pallas_call(
        functools.partial(place_kernel, full_rows * width),
        grid=(blocks // group,),
        out_shape=(
            jax.ShapeDtypeStruct((blocks, tall, width), BF16),
            jax.ShapeDtypeStruct((1, 1), F32),
        ),
        in_specs=[
            pl.BlockSpec((group, high, lanes), lambda i: (i, 0, 0)),
            pl.BlockSpec((group, 1, 1), lambda i: (i, 0, 0)),
        ],
        out_specs=(pl.BlockSpec((group, tall, width), lambda i: (i, 0, 0)), SMEM),
        compiler_params=pltpu.CompilerParams(vmem_limit_bytes=60 * 2**20),
    )(back, hits.astype(jnp.int32).reshape(blocks, 1, 1))


def shift(value, axis, distance):
    n = lax.axis_size(axis)
    return lax.ppermute(value, axis, [(i, (i + distance) % n) for i in range(n)])


def neighbour(value, axis, turn):
    ring, core_n = lax.axis_size(axis), lax.axis_size("core")
    pairs = []
    for at in range(ring):
        for core in range(core_n):
            other = at ^ 1 if (turn + core) % 2 == 0 else ring - 1 - at
            pairs.append((at * core_n + core, other * core_n + core))
    return lax.ppermute(value, (axis, "core"), pairs)


def on_device(grads, owners):
    block = grads[0]
    mats, rows_dev, width = block.shape
    dp_n, y_n, core_n = lax.axis_size("dp"), lax.axis_size("y"), lax.axis_size("core")
    far_n, mid_n, near_n = lax.axis_size("zh"), lax.axis_size("zm"), lax.axis_size("zb")
    mats_dp = mats // dp_n
    full_rows = y_n * far_n * mid_n * near_n * core_n * rows_dev
    core = lax.axis_index("core").astype(jnp.int32).reshape(1)
    mid = lax.axis_index("zm")

    slabs = block.reshape(dp_n * y_n * near_n, mid_n, rows_dev, width)
    slabs = lax.all_to_all(slabs, ("dp", "y", "zb"), 0, 0, tiled=True)
    slabs = slabs.reshape(dp_n, y_n * near_n, mid_n, rows_dev, width)

    def summed(which):
        part = lax.dynamic_index_in_dim(slabs, which, 2, keepdims=False)
        return jnp.sum(part.astype(F32), axis=0).astype(BF16)

    away = shift(summed(1 - mid), "zm", 1)
    here = summed(mid)
    mine = jnp.stack([jnp.where(mid == 0, here, away), jnp.where(mid == 0, away, here)], axis=1)
    mine = mine.reshape(mats_dp * rows_dev, width)
    pieces = [part.reshape(-1, width) for part in (here, away)]
    pieces += [shift(part, "core", 1) for part in pieces]
    total, sent = half_gram(core, pieces)
    cut = HALF // 2 // SPARE * SPARE
    totals = [total[:cut], total[cut:]]
    sents = [sent[:cut], sent[cut:]]
    for turn in range(2):
        came = [neighbour(part, "zh", turn) for part in sents]
        totals = [part + other.astype(F32) for part, other in zip(totals, came)]
        sents = [part.astype(BF16) for part in totals]
    total, sent = jnp.concatenate(totals), jnp.concatenate(sents)
    slab = polynomial(core, total, shift(sent, "core", 1), mine, full_rows, mats_dp)
    back = lax.all_to_all(slab, ("y", "zb", "zm"), 0, 0, tiled=True)

    index = jnp.zeros((), jnp.int32)
    for axis in FSDP:
        index = index * lax.axis_size(axis) + lax.axis_index(axis)
    owned = lax.dynamic_slice_in_dim(owners, lax.axis_index("dp") * mats_dp, mats_dp)
    hits = owned == index - index % core_n
    return place(back, hits, rows_dev, width, full_rows)


def solution(mesh):
    dp_n, fsdp_n = mesh.devices.shape
    shape = (dp_n, 4, fsdp_n // 32, 2, 2, 2)
    grid = Mesh(mesh.devices.reshape(shape), ("dp", *FSDP))
    in_specs = (P("dp", None, FSDP, None), P())
    out_specs = (P("dp", FSDP, None), P("dp", FSDP))
    return jax.shard_map(
        on_device, mesh=grid, in_specs=in_specs, out_specs=out_specs, check_vma=False
    )
```

```python
import functools
import math

import jax
import jax.numpy as jnp
from jax import lax
from jax.experimental import pallas as pl
from jax.experimental.pallas import tpu as pltpu
from jax.sharding import Mesh
from jax.sharding import PartitionSpec as P

COEF_A = 3.4445
COEF_B = -4.775
COEF_C = 2.0315
EPS = 1e-07

BF16 = jnp.bfloat16
F32 = jnp.float32
VMEM = pl.BlockSpec(memory_space=pltpu.VMEM)
SMEM = pl.BlockSpec(memory_space=pltpu.SMEM)
TILE = 256
FSDP = ("y", "zh", "zm", "zb", "core")
LANES = 128
NOTE = 8


def dot(a, b):
    return jnp.dot(a, b, preferred_element_type=F32)


def gram_of(a, b):
    return lax.dot_general(a, b, (((0,), (0,)), ((), ())), preferred_element_type=F32)


def lower(width):
    return [(slice(j, width), slice(j, j + TILE)) for j in range(0, width, TILE)]


def store_symmetric(ref, rows, cols, value):
    ref[rows, cols] = value
    if cols.stop < rows.stop:
        ref[cols, cols.stop : rows.stop] = value[TILE:].T


def indices(shape):
    return (lax.broadcasted_iota(jnp.int32, shape, d) for d in range(2))


def diagonal(block):
    row, col = indices(block.shape)
    return jnp.sum(jnp.where(row == col, block, 0.0), axis=0, keepdims=True)


def merge(one, two):
    row, col = indices(one.shape)
    return jnp.where(row >= col, one, two), diagonal(two)


def split(both, second_diagonal):
    row, col = indices(both.shape)
    other = both.T
    two = jnp.where(row < col, both, jnp.where(row == col, second_diagonal, other))
    return jnp.where(row >= col, both, other), two


SMALL = TILE // 2
SPARE = 16
HALF = 2 * TILE + SMALL // 2 + SPARE


def gram_kernel(core_ref, *refs):
    *pieces, wide_ref, sent_ref, stack = refs
    rows = pieces[0].shape[0]
    for i, piece in enumerate(pieces):
        stack[i * rows : (i + 1) * rows, :] = piece[...]
    first = core_ref[0] == 0
    one, two, three = (stack[:, i * TILE : (i + 1) * TILE] for i in range(3))
    below = gram_of(stack[:, TILE:], one)
    middle = gram_of(stack[:, TILE:], two)
    last = gram_of(three, three)
    corner, corner_diagonal = merge(gram_of(one, one), middle[:TILE])
    tip, tip_diagonal = merge(last[:SMALL, :SMALL], last[SMALL:, SMALL:])

    def store(span, lanes, value):
        wide_ref[span, lanes] = value
        sent_ref[span, lanes] = value.astype(BF16)

    every = slice(0, TILE)
    store(slice(0, TILE), every, jnp.where(first, below[:TILE], middle[TILE:]))
    store(slice(TILE, 2 * TILE), every, jnp.where(first, below[TILE:], corner))
    small = jnp.where(first, tip, last[SMALL:, :SMALL])
    span = slice(2 * TILE, HALF - SPARE)
    store(span, slice(0, SMALL), small[: SMALL // 2])
    store(span, slice(SMALL, TILE), small[SMALL // 2 :])
    span = slice(HALF - SPARE, HALF)
    left, right = corner_diagonal[:, :SMALL], corner_diagonal[:, SMALL:]
    store(span, slice(0, SMALL), jnp.broadcast_to(jnp.where(first, tip_diagonal, left), (SPARE, SMALL)))
    store(span, slice(SMALL, TILE), jnp.broadcast_to(jnp.where(first, 0.0, right), (SPARE, SMALL)))


def half_gram(core, pieces):
    rows, width = pieces[0].shape
    assert width == 3 * TILE
    shape = (HALF, TILE)
    return pl.pallas_call(
        gram_kernel,
        out_shape=(jax.ShapeDtypeStruct(shape, F32), jax.ShapeDtypeStruct(shape, BF16)),
        in_specs=[SMEM] + [VMEM] * len(pieces),
        out_specs=(VMEM, VMEM),
        scratch_shapes=[pltpu.VMEM((len(pieces) * rows, width), BF16)],
        compiler_params=pltpu.CompilerParams(vmem_limit_bytes=32 * 2**20),
        cost_estimate=pl.CostEstimate(
            flops=len(pieces) * rows * width * width,
            bytes_accessed=len(pieces) * rows * width * 2 + shape[0] * TILE * 6,
            transcendentals=0,
        ),
    )(core, *pieces)


def polynomial_kernel(scale, core_ref, *refs):
    own_refs, other_refs, (x_ref, slab_ref, both, wide, g, p, s) = refs[:2], refs[2:4], refs[4:]
    width = g.shape[0]
    core = core_ref[0]
    at = 0
    for own_ref, other_ref in zip(own_refs, other_refs):
        span = slice(at, at + own_ref.shape[0])
        at = span.stop
        own, other = own_ref[...], other_ref[...].astype(F32)
        both[0, span, :] = jnp.where(core == 0, own, other)
        both[1, span, :] = jnp.where(core == 0, other, own)

    def pick(half, span):
        return both[half, span, :]

    def place(i, j, value, size=TILE):
        wide[i * size : i * size + value.shape[0], j * size : j * size + value.shape[1]] = value

    def small(half):
        value = pick(half, slice(2 * TILE, HALF - SPARE))
        return jnp.concatenate([value[:, :SMALL], value[:, SMALL:]], axis=0)

    spare = slice(HALF - SPARE, HALF - SPARE + 8)
    tip_diagonal, corner_diagonal = pick(0, spare)[:1, :SMALL], pick(1, spare)[:1]
    corner, tip = pick(1, slice(TILE, 2 * TILE)), small(0)
    place(1, 0, pick(0, slice(0, TILE)))
    place(2, 0, pick(0, slice(TILE, 2 * TILE)))
    place(2, 1, pick(1, slice(0, TILE)))
    one, two = split(corner, corner_diagonal)
    place(0, 0, one)
    place(1, 1, two)
    one, two = split(tip, tip_diagonal)
    bend = small(1)
    place(4, 4, one, SMALL)
    place(5, 5, two, SMALL)
    place(5, 4, bend, SMALL)
    place(4, 5, bend.T, SMALL)
    trace = sum(
        jnp.sum(part, axis=1, keepdims=True)
        for part in (diagonal(corner), corner_diagonal, diagonal(tip), tip_diagonal)
    )
    norm = jnp.sqrt(trace)
    inv = 1.0 / (norm + EPS)

    for down, cols in lower(width):
        store_symmetric(g, down, cols, (wide[down, cols] * (inv * inv)).astype(BF16))
    for down, cols in lower(width):
        part = COEF_B * g[down, cols].astype(F32) + COEF_C * dot(g[down, :], g[:, cols])
        store_symmetric(p, down, cols, part.astype(BF16))
    for down, cols in lower(width):
        part = dot(g[down, :], p[:, cols])
        wide[down, cols] = (2 * COEF_A) * part + (COEF_A * COEF_A) * g[down, cols].astype(F32)
        store_symmetric(s, down, cols, part.astype(BF16))
    for down, cols in lower(width):
        part = wide[down, cols] + dot(p[down, :], s[:, cols])
        store_symmetric(g, down, cols, part.astype(BF16))
    for down, cols in lower(width):
        part = COEF_B * g[down, cols].astype(F32) + COEF_C * dot(g[down, :], g[:, cols])
        store_symmetric(s, down, cols, part.astype(BF16))

    x = x_ref[...]
    x1 = (inv * (COEF_A * x.astype(F32) + dot(x, p[...]))).astype(BF16)
    update = (scale * (COEF_A * x1.astype(F32) + dot(x1, s[...]))).astype(BF16)
    blocks, high, _ = slab_ref.shape
    tall = update.shape[0] // blocks
    for i in range(width // LANES):
        slab_ref[:, i * tall : (i + 1) * tall, :] = update[:, i * LANES : (i + 1) * LANES].reshape(
            blocks, tall, LANES
        )
    first = norm.astype(BF16).astype(F32)
    second = norm - first
    note = lax.broadcasted_iota(jnp.int32, (NOTE, LANES), 0)
    note = jnp.where(note < NOTE // 2, first, second).astype(BF16)
    slab_ref[:, high - NOTE :, :] = jnp.broadcast_to(note, (blocks, NOTE, LANES))


def polynomial(core, owns, others, x, full_rows, blocks):
    rows, width = x.shape
    mat = pltpu.VMEM((width, width), BF16)
    high = rows // blocks * width // LANES + NOTE
    return pl.pallas_call(
        functools.partial(polynomial_kernel, math.sqrt(full_rows)),
        out_shape=jax.ShapeDtypeStruct((blocks, high, LANES), BF16),
        in_specs=[SMEM] + [VMEM] * 5,
        out_specs=VMEM,
        scratch_shapes=[
            pltpu.VMEM((2, HALF, TILE), F32),
            pltpu.VMEM((width, width), F32),
            mat,
            mat,
            mat,
        ],
        compiler_params=pltpu.CompilerParams(vmem_limit_bytes=32 * 2**20),
        cost_estimate=pl.CostEstimate(
            flops=6 * width**3 + 4 * rows * width * width,
            bytes_accessed=width * width * 3 + rows * width * 4,
            transcendentals=0,
        ),
    )(core, *owns, *others, x)


def place_kernel(count, back_ref, hit_ref, out_ref, rms_ref):
    tall, width = out_ref.shape[1:]
    for i in range(width // LANES):
        out_ref[:, :, i * LANES : (i + 1) * LANES] = back_ref[:, i * tall : (i + 1) * tall, :]
    note = back_ref[:, back_ref.shape[1] - NOTE :, :].astype(F32)
    norms = note[:, :1, :1] + note[:, NOTE // 2 : NOTE // 2 + 1, :1]
    mine = jnp.sum(jnp.where(hit_ref[...] > 0, norms, 0.0)) / math.sqrt(count)
    step = pl.program_id(0)

    @pl.when(step == 0)
    def _():
        rms_ref[0, 0] = mine

    @pl.when(step > 0)
    def _():
        rms_ref[0, 0] = rms_ref[0, 0] + mine


def place(back, hits, tall, width, full_rows):
    blocks, high, lanes = back.shape
    group = blocks // 2
    return pl.pallas_call(
        functools.partial(place_kernel, full_rows * width),
        grid=(blocks // group,),
        out_shape=(
            jax.ShapeDtypeStruct((blocks, tall, width), BF16),
            jax.ShapeDtypeStruct((1, 1), F32),
        ),
        in_specs=[
            pl.BlockSpec((group, high, lanes), lambda i: (i, 0, 0)),
            pl.BlockSpec((group, 1, 1), lambda i: (i, 0, 0)),
        ],
        out_specs=(pl.BlockSpec((group, tall, width), lambda i: (i, 0, 0)), SMEM),
        compiler_params=pltpu.CompilerParams(vmem_limit_bytes=60 * 2**20),
    )(back, hits.astype(jnp.int32).reshape(blocks, 1, 1))


def shift(value, axis, distance):
    n = lax.axis_size(axis)
    return lax.ppermute(value, axis, [(i, (i + distance) % n) for i in range(n)])


def neighbour(value, axis, turn):
    ring, core_n = lax.axis_size(axis), lax.axis_size("core")
    pairs = []
    for at in range(ring):
        for core in range(core_n):
            other = at ^ 1 if (turn + core) % 2 == 0 else ring - 1 - at
            pairs.append((at * core_n + core, other * core_n + core))
    return lax.ppermute(value, (axis, "core"), pairs)


def swap_windows(value):
    z_n = lax.axis_size("zh") * 4
    pairs = []
    for z in range(z_n):
        up = z % 4 // 2
        for core in range(2):
            other = z + 2 if up == core else z - 2
            pairs.append((z * 2 + core, other % z_n * 2 + core))
    return lax.ppermute(value, FSDP[1:], pairs)


def window_groups(fsdp_n):
    z_n = fsdp_n // 8
    return [
        [
            (y * z_n + (first + 2 * (zm + 2 * core * (1 - zm)) + zb) % z_n) * 2 + core
            for y in range(4)
            for zb in range(2)
            for zm in range(2)
        ]
        for first in range(0, z_n, 4)
        for core in range(2)
    ]


def on_device(grads):
    block = grads[0]
    mats, rows_dev, width = block.shape
    dp_n, y_n, core_n = lax.axis_size("dp"), lax.axis_size("y"), lax.axis_size("core")
    far_n, mid_n, near_n = lax.axis_size("zh"), lax.axis_size("zm"), lax.axis_size("zb")
    mats_dp = mats // dp_n
    full_rows = y_n * far_n * mid_n * near_n * core_n * rows_dev
    core = lax.axis_index("core").astype(jnp.int32).reshape(1)
    mid = lax.axis_index("zm")

    slabs = block.reshape(dp_n * y_n * near_n, mid_n, rows_dev, width)
    slabs = lax.all_to_all(slabs, ("dp", "y", "zb"), 0, 0, tiled=True)
    slabs = slabs.reshape(dp_n, y_n * near_n, mid_n, rows_dev, width)

    def summed(which):
        part = lax.dynamic_index_in_dim(slabs, which, 2, keepdims=False)
        return jnp.sum(part.astype(F32), axis=0).astype(BF16)

    away = swap_windows(summed(1 - mid))
    here = summed(mid)
    mine = jnp.stack([jnp.where(mid == 0, here, away), jnp.where(mid == 0, away, here)], axis=1)
    mine = mine.reshape(mats_dp * rows_dev, width)
    pieces = [part.reshape(-1, width) for part in (here, away)]
    pieces += [shift(part, "core", 1) for part in pieces]
    total, sent = half_gram(core, pieces)
    cut = HALF // 2 // SPARE * SPARE
    totals = [total[:cut], total[cut:]]
    sents = [sent[:cut], sent[cut:]]
    for turn in range(2):
        came = [neighbour(part, "zh", turn) for part in sents]
        totals = [part + other.astype(F32) for part, other in zip(totals, came)]
        sents = [part.astype(BF16) for part in totals]
    others = [shift(part, "core", 1) for part in sents]
    slab = polynomial(core, totals, others, mine, full_rows, mats_dp)
    return slab


def placed(slab, owners, rows_dev, width, full_rows):
    groups = window_groups(lax.axis_size("fsdp"))
    back = lax.all_to_all(slab, "fsdp", 0, 0, axis_index_groups=groups, tiled=True)
    mats_dp = back.shape[0]
    index = lax.axis_index("fsdp")
    owned = lax.dynamic_slice_in_dim(owners, lax.axis_index("dp") * mats_dp, mats_dp)
    hits = owned == index - index % 2
    return place(back, hits, rows_dev, width, full_rows)


def solution(mesh):
    dp_n, fsdp_n = mesh.devices.shape
    shape = (dp_n, 4, fsdp_n // 32, 2, 2, 2)
    grid = Mesh(mesh.devices.reshape(shape), ("dp", *FSDP))

    def run(grads, owners):
        full_rows, width = grads.shape[2:]
        slabs = jax.shard_map(
            on_device,
            mesh=grid,
            in_specs=P("dp", None, FSDP, None),
            out_specs=P(("dp", *FSDP)),
            check_vma=False,
        )(grads)
        return jax.shard_map(
            functools.partial(
                placed, rows_dev=full_rows // fsdp_n, width=width, full_rows=full_rows
            ),
            mesh=mesh,
            in_specs=(P(("dp", "fsdp")), P()),
            out_specs=(P("dp", "fsdp", None), P("dp", "fsdp")),
            check_vma=False,
        )(slabs, owners)

    return run
```

```python
import functools
import math

import jax
import jax.numpy as jnp
from jax import lax
from jax.experimental import pallas as pl
from jax.experimental.pallas import tpu as pltpu
from jax.sharding import Mesh
from jax.sharding import PartitionSpec as P

COEF_A = 3.4445
COEF_B = -4.775
COEF_C = 2.0315
EPS = 1e-07

BF16 = jnp.bfloat16
F32 = jnp.float32
VMEM = pl.BlockSpec(memory_space=pltpu.VMEM)
SMEM = pl.BlockSpec(memory_space=pltpu.SMEM)
TILE = 256
FSDP = ("y", "zh", "zm", "zb", "core")
LANES = 128
NOTE = 8


def dot(a, b):
    return jnp.dot(a, b, preferred_element_type=F32)


def gram_of(a, b):
    return lax.dot_general(a, b, (((0,), (0,)), ((), ())), preferred_element_type=F32)


def lower(width):
    return [(slice(j, width), slice(j, j + TILE)) for j in range(0, width, TILE)]


def store_symmetric(ref, rows, cols, value):
    ref[rows, cols] = value
    if cols.stop < rows.stop:
        ref[cols, cols.stop : rows.stop] = value[TILE:].T


def indices(shape):
    return (lax.broadcasted_iota(jnp.int32, shape, d) for d in range(2))


def diagonal(block):
    row, col = indices(block.shape)
    return jnp.sum(jnp.where(row == col, block, 0.0), axis=0, keepdims=True)


def merge(one, two):
    row, col = indices(one.shape)
    return jnp.where(row >= col, one, two), diagonal(two)


def split(both, second_diagonal):
    row, col = indices(both.shape)
    other = both.T
    two = jnp.where(row < col, both, jnp.where(row == col, second_diagonal, other))
    return jnp.where(row >= col, both, other), two


SMALL = TILE // 2
SPARE = 16
HALF = 2 * TILE + SMALL // 2 + SPARE


def gram_kernel(core_ref, *refs):
    *pieces, wide_ref, sent_ref, stack = refs
    rows = pieces[0].shape[0]
    for i, piece in enumerate(pieces):
        stack[i * rows : (i + 1) * rows, :] = piece[...]
    first = core_ref[0] == 0
    one, two, three = (stack[:, i * TILE : (i + 1) * TILE] for i in range(3))
    below = gram_of(stack[:, TILE:], one)
    middle = gram_of(stack[:, TILE:], two)
    last = gram_of(three, three)
    corner, corner_diagonal = merge(gram_of(one, one), middle[:TILE])
    tip, tip_diagonal = merge(last[:SMALL, :SMALL], last[SMALL:, SMALL:])

    def store(span, lanes, value):
        wide_ref[span, lanes] = value
        sent_ref[span, lanes] = value.astype(BF16)

    every = slice(0, TILE)
    store(slice(0, TILE), every, jnp.where(first, below[:TILE], middle[TILE:]))
    store(slice(TILE, 2 * TILE), every, jnp.where(first, below[TILE:], corner))
    small = jnp.where(first, tip, last[SMALL:, :SMALL])
    span = slice(2 * TILE, HALF - SPARE)
    store(span, slice(0, SMALL), small[: SMALL // 2])
    store(span, slice(SMALL, TILE), small[SMALL // 2 :])
    span = slice(HALF - SPARE, HALF)
    left, right = corner_diagonal[:, :SMALL], corner_diagonal[:, SMALL:]
    store(span, slice(0, SMALL), jnp.broadcast_to(jnp.where(first, tip_diagonal, left), (SPARE, SMALL)))
    store(span, slice(SMALL, TILE), jnp.broadcast_to(jnp.where(first, 0.0, right), (SPARE, SMALL)))


def half_gram(core, pieces):
    rows, width = pieces[0].shape
    assert width == 3 * TILE
    shape = (HALF, TILE)
    return pl.pallas_call(
        gram_kernel,
        out_shape=(jax.ShapeDtypeStruct(shape, F32), jax.ShapeDtypeStruct(shape, BF16)),
        in_specs=[SMEM] + [VMEM] * len(pieces),
        out_specs=(VMEM, VMEM),
        scratch_shapes=[pltpu.VMEM((len(pieces) * rows, width), BF16)],
        compiler_params=pltpu.CompilerParams(vmem_limit_bytes=32 * 2**20),
        cost_estimate=pl.CostEstimate(
            flops=len(pieces) * rows * width * width,
            bytes_accessed=len(pieces) * rows * width * 2 + shape[0] * TILE * 6,
            transcendentals=0,
        ),
    )(core, *pieces)


def polynomial_kernel(scale, core_ref, *refs):
    own_refs, other_refs, (x_ref, slab_ref, both, wide, g, p, s) = refs[:2], refs[2:4], refs[4:]
    width = g.shape[0]
    core = core_ref[0]
    at = 0
    for own_ref, other_ref in zip(own_refs, other_refs):
        span = slice(at, at + own_ref.shape[0])
        at = span.stop
        own, other = own_ref[...], other_ref[...].astype(F32)
        both[0, span, :] = jnp.where(core == 0, own, other)
        both[1, span, :] = jnp.where(core == 0, other, own)

    def pick(half, span):
        return both[half, span, :]

    def place(i, j, value, size=TILE):
        wide[i * size : i * size + value.shape[0], j * size : j * size + value.shape[1]] = value

    def small(half):
        value = pick(half, slice(2 * TILE, HALF - SPARE))
        return jnp.concatenate([value[:, :SMALL], value[:, SMALL:]], axis=0)

    spare = slice(HALF - SPARE, HALF - SPARE + 8)
    tip_diagonal, corner_diagonal = pick(0, spare)[:1, :SMALL], pick(1, spare)[:1]
    corner, tip = pick(1, slice(TILE, 2 * TILE)), small(0)
    place(1, 0, pick(0, slice(0, TILE)))
    place(2, 0, pick(0, slice(TILE, 2 * TILE)))
    place(2, 1, pick(1, slice(0, TILE)))
    one, two = split(corner, corner_diagonal)
    place(0, 0, one)
    place(1, 1, two)
    one, two = split(tip, tip_diagonal)
    bend = small(1)
    place(4, 4, one, SMALL)
    place(5, 5, two, SMALL)
    place(5, 4, bend, SMALL)
    place(4, 5, bend.T, SMALL)
    trace = sum(
        jnp.sum(part, axis=1, keepdims=True)
        for part in (diagonal(corner), corner_diagonal, diagonal(tip), tip_diagonal)
    )
    norm = jnp.sqrt(trace)
    inv = 1.0 / (norm + EPS)

    for down, cols in lower(width):
        store_symmetric(g, down, cols, (wide[down, cols] * (inv * inv)).astype(BF16))
    for down, cols in lower(width):
        part = COEF_B * g[down, cols].astype(F32) + COEF_C * dot(g[down, :], g[:, cols])
        store_symmetric(p, down, cols, part.astype(BF16))
    for down, cols in lower(width):
        part = dot(g[down, :], p[:, cols])
        wide[down, cols] = (2 * COEF_A) * part + (COEF_A * COEF_A) * g[down, cols].astype(F32)
        store_symmetric(s, down, cols, part.astype(BF16))
    for down, cols in lower(width):
        part = wide[down, cols] + dot(p[down, :], s[:, cols])
        store_symmetric(g, down, cols, part.astype(BF16))
    for down, cols in lower(width):
        part = COEF_B * g[down, cols].astype(F32) + COEF_C * dot(g[down, :], g[:, cols])
        store_symmetric(s, down, cols, part.astype(BF16))

    x = x_ref[...]
    x1 = (inv * (COEF_A * x.astype(F32) + dot(x, p[...]))).astype(BF16)
    update = (scale * (COEF_A * x1.astype(F32) + dot(x1, s[...]))).astype(BF16)
    blocks, high, _ = slab_ref.shape
    tall = update.shape[0] // blocks
    for i in range(width // LANES):
        slab_ref[:, i * tall : (i + 1) * tall, :] = update[:, i * LANES : (i + 1) * LANES].reshape(
            blocks, tall, LANES
        )
    first = norm.astype(BF16).astype(F32)
    second = norm - first
    note = lax.broadcasted_iota(jnp.int32, (NOTE, LANES), 0)
    note = jnp.where(note < NOTE // 2, first, second).astype(BF16)
    slab_ref[:, high - NOTE :, :] = jnp.broadcast_to(note, (blocks, NOTE, LANES))


def polynomial(core, owns, others, x, full_rows, blocks):
    rows, width = x.shape
    mat = pltpu.VMEM((width, width), BF16)
    high = rows // blocks * width // LANES + NOTE
    return pl.pallas_call(
        functools.partial(polynomial_kernel, math.sqrt(full_rows)),
        out_shape=jax.ShapeDtypeStruct((blocks, high, LANES), BF16),
        in_specs=[SMEM] + [VMEM] * 5,
        out_specs=VMEM,
        scratch_shapes=[
            pltpu.VMEM((2, HALF, TILE), F32),
            pltpu.VMEM((width, width), F32),
            mat,
            mat,
            mat,
        ],
        compiler_params=pltpu.CompilerParams(vmem_limit_bytes=32 * 2**20),
        cost_estimate=pl.CostEstimate(
            flops=6 * width**3 + 4 * rows * width * width,
            bytes_accessed=width * width * 3 + rows * width * 4,
            transcendentals=0,
        ),
    )(core, *owns, *others, x)


def place_kernel(count, back_ref, hit_ref, out_ref, rms_ref):
    tall, width = out_ref.shape[1:]
    for i in range(width // LANES):
        out_ref[:, :, i * LANES : (i + 1) * LANES] = back_ref[:, i * tall : (i + 1) * tall, :]
    note = back_ref[:, back_ref.shape[1] - NOTE :, :].astype(F32)
    norms = note[:, :1, :1] + note[:, NOTE // 2 : NOTE // 2 + 1, :1]
    mine = jnp.sum(jnp.where(hit_ref[...] > 0, norms, 0.0)) / math.sqrt(count)
    step = pl.program_id(0)

    @pl.when(step == 0)
    def _():
        rms_ref[0, 0] = mine

    @pl.when(step > 0)
    def _():
        rms_ref[0, 0] = rms_ref[0, 0] + mine


def place(back, hits, tall, width, full_rows):
    blocks, high, lanes = back.shape
    group = blocks // 2
    return pl.pallas_call(
        functools.partial(place_kernel, full_rows * width),
        grid=(blocks // group,),
        out_shape=(
            jax.ShapeDtypeStruct((blocks, tall, width), BF16),
            jax.ShapeDtypeStruct((1, 1), F32),
        ),
        in_specs=[
            pl.BlockSpec((group, high, lanes), lambda i: (i, 0, 0)),
            pl.BlockSpec((group, 1, 1), lambda i: (i, 0, 0)),
        ],
        out_specs=(pl.BlockSpec((group, tall, width), lambda i: (i, 0, 0)), SMEM),
        compiler_params=pltpu.CompilerParams(vmem_limit_bytes=60 * 2**20),
    )(back, hits.astype(jnp.int32).reshape(blocks, 1, 1))


def shift(value, axis, distance):
    n = lax.axis_size(axis)
    return lax.ppermute(value, axis, [(i, (i + distance) % n) for i in range(n)])


def neighbour(value, axis, turn):
    ring, core_n = lax.axis_size(axis), lax.axis_size("core")
    pairs = []
    for at in range(ring):
        for core in range(core_n):
            other = at ^ 1 if (turn + core) % 2 == 0 else ring - 1 - at
            pairs.append((at * core_n + core, other * core_n + core))
    return lax.ppermute(value, (axis, "core"), pairs)


def swap_windows(value):
    z_n = lax.axis_size("zh") * 4
    pairs = []
    for z in range(z_n):
        up = z % 4 // 2
        for core in range(2):
            other = z + 2 if up == core else z - 2
            pairs.append((z * 2 + core, other % z_n * 2 + core))
    return lax.ppermute(value, FSDP[1:], pairs)


def window_groups(fsdp_n):
    z_n = fsdp_n // 8
    return [
        [
            (y * z_n + (first + 2 * (zm + 2 * core * (1 - zm)) + zb) % z_n) * 2 + core
            for y in range(4)
            for zb in range(2)
            for zm in range(2)
        ]
        for first in range(0, z_n, 4)
        for core in range(2)
    ]


def on_device(grads):
    block = grads[0]
    mats, rows_dev, width = block.shape
    dp_n, y_n, core_n = lax.axis_size("dp"), lax.axis_size("y"), lax.axis_size("core")
    far_n, mid_n, near_n = lax.axis_size("zh"), lax.axis_size("zm"), lax.axis_size("zb")
    mats_dp = mats // dp_n
    full_rows = y_n * far_n * mid_n * near_n * core_n * rows_dev
    core = lax.axis_index("core").astype(jnp.int32).reshape(1)
    mid = lax.axis_index("zm")

    slabs = block.reshape(dp_n * y_n * near_n, mid_n, rows_dev, width)
    slabs = lax.all_to_all(slabs, ("dp", "y", "zb"), 0, 0, tiled=True)
    slabs = slabs.reshape(dp_n, y_n * near_n, mid_n, rows_dev, width)

    def summed(which):
        part = lax.dynamic_index_in_dim(slabs, which, 2, keepdims=False)
        return sum(part[i].astype(F32) for i in range(dp_n)).astype(BF16)

    gone, here = lax.optimization_barrier((summed(1 - mid), summed(mid)))
    away = swap_windows(gone)
    mine = jnp.stack([jnp.where(mid == 0, here, away), jnp.where(mid == 0, away, here)], axis=1)
    mine = mine.reshape(mats_dp * rows_dev, width)
    pieces = [part.reshape(-1, width) for part in (here, away)]
    pieces += [shift(part, "core", 1) for part in pieces]
    total, sent = half_gram(core, pieces)
    cut = HALF // 2 // SPARE * SPARE
    totals = [total[:cut], total[cut:]]
    sents = [sent[:cut], sent[cut:]]
    for turn in range(2):
        came = [neighbour(part, "zh", turn) for part in sents]
        totals = [part + other.astype(F32) for part, other in zip(totals, came)]
        sents = [part.astype(BF16) for part in totals]
    others = [shift(part, "core", 1) for part in sents]
    slab = polynomial(core, totals, others, mine, full_rows, mats_dp)
    return slab


def placed(slab, owners, rows_dev, width, full_rows):
    groups = window_groups(lax.axis_size("fsdp"))
    back = lax.all_to_all(slab, "fsdp", 0, 0, axis_index_groups=groups, tiled=True)
    mats_dp = back.shape[0]
    index = lax.axis_index("fsdp")
    owned = lax.dynamic_slice_in_dim(owners, lax.axis_index("dp") * mats_dp, mats_dp)
    hits = owned == index - index % 2
    return place(back, hits, rows_dev, width, full_rows)


def solution(mesh):
    dp_n, fsdp_n = mesh.devices.shape
    shape = (dp_n, 4, fsdp_n // 32, 2, 2, 2)
    grid = Mesh(mesh.devices.reshape(shape), ("dp", *FSDP))

    def run(grads, owners):
        full_rows, width = grads.shape[2:]
        slabs = jax.shard_map(
            on_device,
            mesh=grid,
            in_specs=P("dp", None, FSDP, None),
            out_specs=P(("dp", *FSDP)),
            check_vma=False,
        )(grads)
        return jax.shard_map(
            functools.partial(
                placed, rows_dev=full_rows // fsdp_n, width=width, full_rows=full_rows
            ),
            mesh=mesh,
            in_specs=(P(("dp", "fsdp")), P()),
            out_specs=(P("dp", "fsdp", None), P("dp", "fsdp")),
            check_vma=False,
        )(slabs, owners)

    return run
```

```python
import functools
import math

import jax
import jax.numpy as jnp
from jax import lax
from jax.experimental import pallas as pl
from jax.experimental.pallas import tpu as pltpu
from jax.sharding import Mesh
from jax.sharding import PartitionSpec as P

COEF_A = 3.4445
COEF_B = -4.775
COEF_C = 2.0315
EPS = 1e-07

BF16 = jnp.bfloat16
F32 = jnp.float32
VMEM = pl.BlockSpec(memory_space=pltpu.VMEM)
SMEM = pl.BlockSpec(memory_space=pltpu.SMEM)
TILE = 256
FSDP = ("y", "zh", "zm", "zb", "core")
LANES = 128
NOTE = 16


def dot(a, b):
    return jnp.dot(a, b, preferred_element_type=F32)


def gram_of(a, b):
    return lax.dot_general(a, b, (((0,), (0,)), ((), ())), preferred_element_type=F32)


def lower(width):
    return [(slice(j, width), slice(j, j + TILE)) for j in range(0, width, TILE)]


def store_symmetric(ref, rows, cols, value):
    ref[rows, cols] = value
    if cols.stop < rows.stop:
        ref[cols, cols.stop : rows.stop] = value[TILE:].T


def indices(shape):
    return (lax.broadcasted_iota(jnp.int32, shape, d) for d in range(2))


def diagonal(block):
    row, col = indices(block.shape)
    return jnp.sum(jnp.where(row == col, block, 0.0), axis=0, keepdims=True)


def merge(one, two):
    row, col = indices(one.shape)
    return jnp.where(row >= col, one, two), diagonal(two)


def split(both, second_diagonal):
    row, col = indices(both.shape)
    other = both.T
    two = jnp.where(row < col, both, jnp.where(row == col, second_diagonal, other))
    return jnp.where(row >= col, both, other), two


SMALL = TILE // 2
SPARE = 16
HALF = 2 * TILE + SMALL // 2 + SPARE


def gram_kernel(core_ref, *refs):
    *pieces, wide_ref, sent_ref, stack = refs
    rows = pieces[0].shape[0]
    for i, piece in enumerate(pieces):
        stack[i * rows : (i + 1) * rows, :] = piece[...]
    first = core_ref[0] == 0
    one, two, three = (stack[:, i * TILE : (i + 1) * TILE] for i in range(3))
    below = gram_of(stack[:, TILE:], one)
    middle = gram_of(stack[:, TILE:], two)
    last = gram_of(three, three)
    corner, corner_diagonal = merge(gram_of(one, one), middle[:TILE])
    tip, tip_diagonal = merge(last[:SMALL, :SMALL], last[SMALL:, SMALL:])

    def store(span, lanes, value):
        wide_ref[span, lanes] = value
        sent_ref[span, lanes] = value.astype(BF16)

    every = slice(0, TILE)
    store(slice(0, TILE), every, jnp.where(first, below[:TILE], middle[TILE:]))
    store(slice(TILE, 2 * TILE), every, jnp.where(first, below[TILE:], corner))
    small = jnp.where(first, tip, last[SMALL:, :SMALL])
    span = slice(2 * TILE, HALF - SPARE)
    store(span, slice(0, SMALL), small[: SMALL // 2])
    store(span, slice(SMALL, TILE), small[SMALL // 2 :])
    span = slice(HALF - SPARE, HALF)
    left, right = corner_diagonal[:, :SMALL], corner_diagonal[:, SMALL:]
    store(span, slice(0, SMALL), jnp.broadcast_to(jnp.where(first, tip_diagonal, left), (SPARE, SMALL)))
    store(span, slice(SMALL, TILE), jnp.broadcast_to(jnp.where(first, 0.0, right), (SPARE, SMALL)))


def half_gram(core, pieces):
    rows, width = pieces[0].shape
    assert width == 3 * TILE
    shape = (HALF, TILE)
    return pl.pallas_call(
        gram_kernel,
        out_shape=(jax.ShapeDtypeStruct(shape, F32), jax.ShapeDtypeStruct(shape, BF16)),
        in_specs=[SMEM] + [VMEM] * len(pieces),
        out_specs=(VMEM, VMEM),
        scratch_shapes=[pltpu.VMEM((len(pieces) * rows, width), BF16)],
        compiler_params=pltpu.CompilerParams(vmem_limit_bytes=32 * 2**20),
        cost_estimate=pl.CostEstimate(
            flops=len(pieces) * rows * width * width,
            bytes_accessed=len(pieces) * rows * width * 2 + shape[0] * TILE * 6,
            transcendentals=0,
        ),
    )(core, *pieces)


def polynomial_kernel(scale, core_ref, *refs):
    own_refs, other_refs, (x_ref, slab_ref, both, wide, g, p, s) = refs[:2], refs[2:4], refs[4:]
    width = g.shape[0]
    core = core_ref[0]
    at = 0
    for own_ref, other_ref in zip(own_refs, other_refs):
        span = slice(at, at + own_ref.shape[0])
        at = span.stop
        own, other = own_ref[...], other_ref[...].astype(F32)
        both[0, span, :] = jnp.where(core == 0, own, other)
        both[1, span, :] = jnp.where(core == 0, other, own)

    def pick(half, span):
        return both[half, span, :]

    def place(i, j, value, size=TILE):
        wide[i * size : i * size + value.shape[0], j * size : j * size + value.shape[1]] = value

    def small(half):
        value = pick(half, slice(2 * TILE, HALF - SPARE))
        return jnp.concatenate([value[:, :SMALL], value[:, SMALL:]], axis=0)

    spare = slice(HALF - SPARE, HALF - SPARE + 8)
    tip_diagonal, corner_diagonal = pick(0, spare)[:1, :SMALL], pick(1, spare)[:1]
    corner, tip = pick(1, slice(TILE, 2 * TILE)), small(0)
    place(1, 0, pick(0, slice(0, TILE)))
    place(2, 0, pick(0, slice(TILE, 2 * TILE)))
    place(2, 1, pick(1, slice(0, TILE)))
    one, two = split(corner, corner_diagonal)
    place(0, 0, one)
    place(1, 1, two)
    one, two = split(tip, tip_diagonal)
    bend = small(1)
    place(4, 4, one, SMALL)
    place(5, 5, two, SMALL)
    place(5, 4, bend, SMALL)
    place(4, 5, bend.T, SMALL)
    trace = sum(
        jnp.sum(part, axis=1, keepdims=True)
        for part in (diagonal(corner), corner_diagonal, diagonal(tip), tip_diagonal)
    )
    norm = jnp.sqrt(trace)
    inv = 1.0 / (norm + EPS)

    for down, cols in lower(width):
        store_symmetric(g, down, cols, (wide[down, cols] * (inv * inv)).astype(BF16))
    for down, cols in lower(width):
        part = COEF_B * g[down, cols].astype(F32) + COEF_C * dot(g[down, :], g[:, cols])
        store_symmetric(p, down, cols, part.astype(BF16))
    for down, cols in lower(width):
        part = dot(g[down, :], p[:, cols])
        wide[down, cols] = (2 * COEF_A) * part + (COEF_A * COEF_A) * g[down, cols].astype(F32)
        store_symmetric(s, down, cols, part.astype(BF16))
    for down, cols in lower(width):
        part = wide[down, cols] + dot(p[down, :], s[:, cols])
        store_symmetric(g, down, cols, part.astype(BF16))
    for down, cols in lower(width):
        part = COEF_B * g[down, cols].astype(F32) + COEF_C * dot(g[down, :], g[:, cols])
        store_symmetric(s, down, cols, part.astype(BF16))

    x = x_ref[...]
    x1 = (inv * (COEF_A * x.astype(F32) + dot(x, p[...]))).astype(BF16)
    update = (scale * (COEF_A * x1.astype(F32) + dot(x1, s[...]))).astype(BF16)
    blocks, high, _ = slab_ref.shape
    tall = update.shape[0] // blocks
    for i in range(width // LANES):
        slab_ref[:, i * tall : (i + 1) * tall, :] = update[:, i * LANES : (i + 1) * LANES].reshape(
            blocks, tall, LANES
        )
    first = norm.astype(BF16).astype(F32)
    second = norm - first
    note = lax.broadcasted_iota(jnp.int32, (NOTE, LANES), 0)
    note = jnp.where(note < NOTE // 2, first, second).astype(BF16)
    slab_ref[:, high - NOTE :, :] = jnp.broadcast_to(note, (blocks, NOTE, LANES))


def polynomial(core, owns, others, x, full_rows, blocks):
    rows, width = x.shape
    mat = pltpu.VMEM((width, width), BF16)
    high = rows // blocks * width // LANES + NOTE
    return pl.pallas_call(
        functools.partial(polynomial_kernel, math.sqrt(full_rows)),
        out_shape=jax.ShapeDtypeStruct((blocks, high, LANES), BF16),
        in_specs=[SMEM] + [VMEM] * 5,
        out_specs=VMEM,
        scratch_shapes=[
            pltpu.VMEM((2, HALF, TILE), F32),
            pltpu.VMEM((width, width), F32),
            mat,
            mat,
            mat,
        ],
        compiler_params=pltpu.CompilerParams(vmem_limit_bytes=32 * 2**20),
        cost_estimate=pl.CostEstimate(
            flops=6 * width**3 + 4 * rows * width * width,
            bytes_accessed=width * width * 3 + rows * width * 4,
            transcendentals=0,
        ),
    )(core, *owns, *others, x)


def place_kernel(count, back_ref, hit_ref, out_ref, rms_ref):
    tall, width = out_ref.shape[1:]
    for i in range(width // LANES):
        out_ref[:, :, i * LANES : (i + 1) * LANES] = back_ref[:, i * tall : (i + 1) * tall, :]
    note = back_ref[:, back_ref.shape[1] - NOTE :, :].astype(F32)
    norms = note[:, :1, :1] + note[:, NOTE // 2 : NOTE // 2 + 1, :1]
    mine = jnp.sum(jnp.where(hit_ref[...] > 0, norms, 0.0)) / math.sqrt(count)
    step = pl.program_id(0)

    @pl.when(step == 0)
    def _():
        rms_ref[0, 0] = mine

    @pl.when(step > 0)
    def _():
        rms_ref[0, 0] = rms_ref[0, 0] + mine


def place(back, hits, tall, width, full_rows):
    blocks, high, lanes = back.shape
    group = blocks // 2
    return pl.pallas_call(
        functools.partial(place_kernel, full_rows * width),
        grid=(blocks // group,),
        out_shape=(
            jax.ShapeDtypeStruct((blocks, tall, width), BF16),
            jax.ShapeDtypeStruct((1, 1), F32),
        ),
        in_specs=[
            pl.BlockSpec((group, high, lanes), lambda i: (i, 0, 0)),
            pl.BlockSpec((group, 1, 1), lambda i: (i, 0, 0)),
        ],
        out_specs=(pl.BlockSpec((group, tall, width), lambda i: (i, 0, 0)), SMEM),
        compiler_params=pltpu.CompilerParams(vmem_limit_bytes=60 * 2**20),
    )(back, hits.astype(jnp.int32).reshape(blocks, 1, 1))


def shift(value, axis, distance):
    n = lax.axis_size(axis)
    return lax.ppermute(value, axis, [(i, (i + distance) % n) for i in range(n)])


def neighbour(value, axis, turn):
    ring, core_n = lax.axis_size(axis), lax.axis_size("core")
    pairs = []
    for at in range(ring):
        for core in range(core_n):
            other = at ^ 1 if (turn + core) % 2 == 0 else ring - 1 - at
            pairs.append((at * core_n + core, other * core_n + core))
    return lax.ppermute(value, (axis, "core"), pairs)


def swap_windows(value):
    z_n = lax.axis_size("zh") * 4
    pairs = []
    for z in range(z_n):
        up = z % 4 // 2
        for core in range(2):
            other = z + 2 if up == core else z - 2
            pairs.append((z * 2 + core, other % z_n * 2 + core))
    return lax.ppermute(value, FSDP[1:], pairs)


def window_groups(fsdp_n):
    z_n = fsdp_n // 8
    return [
        [
            (y * z_n + (first + 2 * (zm + 2 * core * (1 - zm)) + zb) % z_n) * 2 + core
            for y in range(4)
            for zb in range(2)
            for zm in range(2)
        ]
        for first in range(0, z_n, 4)
        for core in range(2)
    ]


def on_device(grads):
    block = grads[0]
    mats, rows_dev, width = block.shape
    dp_n, y_n, core_n = lax.axis_size("dp"), lax.axis_size("y"), lax.axis_size("core")
    far_n, mid_n, near_n = lax.axis_size("zh"), lax.axis_size("zm"), lax.axis_size("zb")
    mats_dp = mats // dp_n
    full_rows = y_n * far_n * mid_n * near_n * core_n * rows_dev
    core = lax.axis_index("core").astype(jnp.int32).reshape(1)
    mid = lax.axis_index("zm")

    slabs = block.reshape(dp_n * y_n * near_n, mid_n, rows_dev, width)
    slabs = lax.all_to_all(slabs, ("dp", "y", "zb"), 0, 0, tiled=True)
    slabs = slabs.reshape(dp_n, y_n * near_n, mid_n, rows_dev, width)

    def summed(which):
        part = lax.dynamic_index_in_dim(slabs, which, 2, keepdims=False)
        return sum(part[i].astype(F32) for i in range(dp_n)).astype(BF16)

    gone, here = lax.optimization_barrier((summed(1 - mid), summed(mid)))
    away = swap_windows(gone)
    mine = jnp.stack([jnp.where(mid == 0, here, away), jnp.where(mid == 0, away, here)], axis=1)
    mine = mine.reshape(mats_dp * rows_dev, width)
    pieces = [part.reshape(-1, width) for part in (here, away)]
    pieces += [shift(part, "core", 1) for part in pieces]
    total, sent = half_gram(core, pieces)
    cut = HALF // 2 // SPARE * SPARE
    totals = [total[:cut], total[cut:]]
    sents = [sent[:cut], sent[cut:]]
    for turn in range(2):
        came = [neighbour(part, "zh", turn) for part in sents]
        totals = [part + other.astype(F32) for part, other in zip(totals, came)]
        sents = [part.astype(BF16) for part in totals]
    others = [shift(part, "core", 1) for part in sents]
    slab = polynomial(core, totals, others, mine, full_rows, mats_dp)
    return slab


def placed(slab, owners, rows_dev, width, full_rows):
    groups = window_groups(lax.axis_size("fsdp"))
    back = lax.all_to_all(slab, "fsdp", 0, 0, axis_index_groups=groups, tiled=True)
    mats_dp = back.shape[0]
    index = lax.axis_index("fsdp")
    owned = lax.dynamic_slice_in_dim(owners, lax.axis_index("dp") * mats_dp, mats_dp)
    hits = owned == index - index % 2
    return place(back, hits, rows_dev, width, full_rows)


def solution(mesh):
    dp_n, fsdp_n = mesh.devices.shape
    shape = (dp_n, 4, fsdp_n // 32, 2, 2, 2)
    grid = Mesh(mesh.devices.reshape(shape), ("dp", *FSDP))

    def run(grads, owners):
        full_rows, width = grads.shape[2:]
        slabs = jax.shard_map(
            on_device,
            mesh=grid,
            in_specs=P("dp", None, FSDP, None),
            out_specs=P(("dp", *FSDP)),
            check_vma=False,
        )(grads)
        return jax.shard_map(
            functools.partial(
                placed, rows_dev=full_rows // fsdp_n, width=width, full_rows=full_rows
            ),
            mesh=mesh,
            in_specs=(P(("dp", "fsdp")), P()),
            out_specs=(P("dp", "fsdp", None), P("dp", "fsdp")),
            check_vma=False,
        )(slabs, owners)

    return run
```

```python
import functools
import math

import jax
import jax.numpy as jnp
from jax import lax
from jax.experimental import pallas as pl
from jax.experimental.pallas import tpu as pltpu
from jax.sharding import Mesh
from jax.sharding import PartitionSpec as P

COEF_A = 3.4445
COEF_B = -4.775
COEF_C = 2.0315
EPS = 1e-07

BF16 = jnp.bfloat16
F32 = jnp.float32
VMEM = pl.BlockSpec(memory_space=pltpu.VMEM)
SMEM = pl.BlockSpec(memory_space=pltpu.SMEM)
TILE = 256
FSDP = ("y", "zh", "zm", "zb", "core")
LANES = 128
NOTE = 8


def dot(a, b):
    return jnp.dot(a, b, preferred_element_type=F32)


def gram_of(a, b):
    return lax.dot_general(a, b, (((0,), (0,)), ((), ())), preferred_element_type=F32)


def lower(width):
    return [(slice(j, width), slice(j, j + TILE)) for j in range(0, width, TILE)]


def store_symmetric(ref, rows, cols, value):
    ref[rows, cols] = value
    if cols.stop < rows.stop:
        ref[cols, cols.stop : rows.stop] = value[TILE:].T


def indices(shape):
    return (lax.broadcasted_iota(jnp.int32, shape, d) for d in range(2))


def diagonal(block):
    row, col = indices(block.shape)
    return jnp.sum(jnp.where(row == col, block, 0.0), axis=0, keepdims=True)


def merge(one, two):
    row, col = indices(one.shape)
    return jnp.where(row >= col, one, two), diagonal(two)


def split(both, second_diagonal):
    row, col = indices(both.shape)
    other = both.T
    two = jnp.where(row < col, both, jnp.where(row == col, second_diagonal, other))
    return jnp.where(row >= col, both, other), two


SMALL = TILE // 2
SPARE = 16
HALF = 2 * TILE + SMALL // 2 + SPARE


def gram_kernel(core_ref, *refs):
    *pieces, wide_ref, sent_ref, stack = refs
    rows = pieces[0].shape[0]
    for i, piece in enumerate(pieces):
        stack[i * rows : (i + 1) * rows, :] = piece[...]
    first = core_ref[0] == 0
    one, two, three = (stack[:, i * TILE : (i + 1) * TILE] for i in range(3))
    below = gram_of(stack[:, TILE:], one)
    middle = gram_of(stack[:, TILE:], two)
    last = gram_of(three, three)
    corner, corner_diagonal = merge(gram_of(one, one), middle[:TILE])
    tip, tip_diagonal = merge(last[:SMALL, :SMALL], last[SMALL:, SMALL:])

    def store(span, lanes, value):
        wide_ref[span, lanes] = value
        sent_ref[span, lanes] = value.astype(BF16)

    every = slice(0, TILE)
    store(slice(0, TILE), every, jnp.where(first, below[:TILE], middle[TILE:]))
    store(slice(TILE, 2 * TILE), every, jnp.where(first, below[TILE:], corner))
    small = jnp.where(first, tip, last[SMALL:, :SMALL])
    span = slice(2 * TILE, HALF - SPARE)
    store(span, slice(0, SMALL), small[: SMALL // 2])
    store(span, slice(SMALL, TILE), small[SMALL // 2 :])
    span = slice(HALF - SPARE, HALF)
    left, right = corner_diagonal[:, :SMALL], corner_diagonal[:, SMALL:]
    store(span, slice(0, SMALL), jnp.broadcast_to(jnp.where(first, tip_diagonal, left), (SPARE, SMALL)))
    store(span, slice(SMALL, TILE), jnp.broadcast_to(jnp.where(first, 0.0, right), (SPARE, SMALL)))


def half_gram(core, pieces):
    rows, width = pieces[0].shape
    assert width == 3 * TILE
    shape = (HALF, TILE)
    return pl.pallas_call(
        gram_kernel,
        out_shape=(jax.ShapeDtypeStruct(shape, F32), jax.ShapeDtypeStruct(shape, BF16)),
        in_specs=[SMEM] + [VMEM] * len(pieces),
        out_specs=(VMEM, VMEM),
        scratch_shapes=[pltpu.VMEM((len(pieces) * rows, width), BF16)],
        compiler_params=pltpu.CompilerParams(vmem_limit_bytes=32 * 2**20),
        cost_estimate=pl.CostEstimate(
            flops=len(pieces) * rows * width * width,
            bytes_accessed=len(pieces) * rows * width * 2 + shape[0] * TILE * 6,
            transcendentals=0,
        ),
    )(core, *pieces)


def polynomial_kernel(scale, core_ref, *refs):
    own_refs, other_refs, (x_ref, slab_ref, both, wide, g, p, s) = refs[:2], refs[2:4], refs[4:]
    width = g.shape[0]
    core = core_ref[0]
    at = 0
    for own_ref, other_ref in zip(own_refs, other_refs):
        span = slice(at, at + own_ref.shape[0])
        at = span.stop
        own, other = own_ref[...], other_ref[...].astype(F32)
        both[0, span, :] = jnp.where(core == 0, own, other)
        both[1, span, :] = jnp.where(core == 0, other, own)

    def pick(half, span):
        return both[half, span, :]

    def place(i, j, value, size=TILE):
        wide[i * size : i * size + value.shape[0], j * size : j * size + value.shape[1]] = value

    def small(half):
        value = pick(half, slice(2 * TILE, HALF - SPARE))
        return jnp.concatenate([value[:, :SMALL], value[:, SMALL:]], axis=0)

    spare = slice(HALF - SPARE, HALF - SPARE + 8)
    tip_diagonal, corner_diagonal = pick(0, spare)[:1, :SMALL], pick(1, spare)[:1]
    corner, tip = pick(1, slice(TILE, 2 * TILE)), small(0)
    place(1, 0, pick(0, slice(0, TILE)))
    place(2, 0, pick(0, slice(TILE, 2 * TILE)))
    place(2, 1, pick(1, slice(0, TILE)))
    one, two = split(corner, corner_diagonal)
    place(0, 0, one)
    place(1, 1, two)
    one, two = split(tip, tip_diagonal)
    bend = small(1)
    place(4, 4, one, SMALL)
    place(5, 5, two, SMALL)
    place(5, 4, bend, SMALL)
    place(4, 5, bend.T, SMALL)
    trace = sum(
        jnp.sum(part, axis=1, keepdims=True)
        for part in (diagonal(corner), corner_diagonal, diagonal(tip), tip_diagonal)
    )
    norm = jnp.sqrt(trace)
    inv = 1.0 / (norm + EPS)

    for down, cols in lower(width):
        store_symmetric(g, down, cols, (wide[down, cols] * (inv * inv)).astype(BF16))
    for down, cols in lower(width):
        part = COEF_B * g[down, cols].astype(F32) + COEF_C * dot(g[down, :], g[:, cols])
        store_symmetric(p, down, cols, part.astype(BF16))
    for down, cols in lower(width):
        part = dot(g[down, :], p[:, cols])
        wide[down, cols] = (2 * COEF_A) * part + (COEF_A * COEF_A) * g[down, cols].astype(F32)
        store_symmetric(s, down, cols, part.astype(BF16))
    for down, cols in lower(width):
        part = wide[down, cols] + dot(p[down, :], s[:, cols])
        store_symmetric(g, down, cols, part.astype(BF16))
    for down, cols in lower(width):
        part = COEF_B * g[down, cols].astype(F32) + COEF_C * dot(g[down, :], g[:, cols])
        store_symmetric(s, down, cols, part.astype(BF16))

    x = x_ref[...]
    x1 = (inv * (COEF_A * x.astype(F32) + dot(x, p[...]))).astype(BF16)
    update = (scale * (COEF_A * x1.astype(F32) + dot(x1, s[...]))).astype(BF16)
    blocks, high, _ = slab_ref.shape
    tall = update.shape[0] // blocks
    for i in range(width // LANES):
        slab_ref[:, i * tall : (i + 1) * tall, :] = update[:, i * LANES : (i + 1) * LANES].reshape(
            blocks, tall, LANES
        )
    first = norm.astype(BF16).astype(F32)
    second = norm - first
    note = lax.broadcasted_iota(jnp.int32, (NOTE, LANES), 0)
    note = jnp.where(note < NOTE // 2, first, second).astype(BF16)
    slab_ref[:, high - NOTE :, :] = jnp.broadcast_to(note, (blocks, NOTE, LANES))


def polynomial(core, owns, others, x, full_rows, blocks):
    rows, width = x.shape
    mat = pltpu.VMEM((width, width), BF16)
    high = rows // blocks * width // LANES + NOTE
    return pl.pallas_call(
        functools.partial(polynomial_kernel, math.sqrt(full_rows)),
        out_shape=jax.ShapeDtypeStruct((blocks, high, LANES), BF16),
        in_specs=[SMEM] + [VMEM] * 5,
        out_specs=VMEM,
        scratch_shapes=[
            pltpu.VMEM((2, HALF, TILE), F32),
            pltpu.VMEM((width, width), F32),
            mat,
            mat,
            mat,
        ],
        compiler_params=pltpu.CompilerParams(vmem_limit_bytes=32 * 2**20),
        cost_estimate=pl.CostEstimate(
            flops=6 * width**3 + 4 * rows * width * width,
            bytes_accessed=width * width * 3 + rows * width * 4,
            transcendentals=0,
        ),
    )(core, *owns, *others, x)


def place_kernel(count, back_ref, hit_ref, out_ref, rms_ref):
    tall, width = out_ref.shape[1:]
    for i in range(width // LANES):
        out_ref[:, :, i * LANES : (i + 1) * LANES] = back_ref[:, i * tall : (i + 1) * tall, :]
    note = back_ref[:, back_ref.shape[1] - NOTE :, :].astype(F32)
    norms = note[:, :1, :1] + note[:, NOTE // 2 : NOTE // 2 + 1, :1]
    mine = jnp.sum(jnp.where(hit_ref[...] > 0, norms, 0.0)) / math.sqrt(count)
    step = pl.program_id(0)

    @pl.when(step == 0)
    def _():
        rms_ref[0, 0] = mine

    @pl.when(step > 0)
    def _():
        rms_ref[0, 0] = rms_ref[0, 0] + mine


def place(back, hits, tall, width, full_rows):
    blocks, high, lanes = back.shape
    group = blocks // 2
    return pl.pallas_call(
        functools.partial(place_kernel, full_rows * width),
        grid=(blocks // group,),
        out_shape=(
            jax.ShapeDtypeStruct((blocks, tall, width), BF16),
            jax.ShapeDtypeStruct((1, 1), F32),
        ),
        in_specs=[
            pl.BlockSpec((group, high, lanes), lambda i: (i, 0, 0)),
            pl.BlockSpec((group, 1, 1), lambda i: (i, 0, 0)),
        ],
        out_specs=(pl.BlockSpec((group, tall, width), lambda i: (i, 0, 0)), SMEM),
        compiler_params=pltpu.CompilerParams(vmem_limit_bytes=60 * 2**20),
    )(back, hits.astype(jnp.int32).reshape(blocks, 1, 1))


def shift(value, axis, distance):
    n = lax.axis_size(axis)
    return lax.ppermute(value, axis, [(i, (i + distance) % n) for i in range(n)])


def neighbour(value, axis, turn):
    ring, core_n = lax.axis_size(axis), lax.axis_size("core")
    pairs = []
    for at in range(ring):
        for core in range(core_n):
            other = at ^ 1 if (turn + core) % 2 == 0 else ring - 1 - at
            pairs.append((at * core_n + core, other * core_n + core))
    return lax.ppermute(value, (axis, "core"), pairs)


def swap_windows(value):
    z_n = lax.axis_size("zh") * 4
    pairs = []
    for z in range(z_n):
        up = z % 4 // 2
        for core in range(2):
            other = z + 2 if up == core else z - 2
            pairs.append((z * 2 + core, other % z_n * 2 + core))
    return lax.ppermute(value, FSDP[1:], pairs)


def window_groups(fsdp_n):
    z_n = fsdp_n // 8
    return [
        [
            (y * z_n + (first + 2 * (zm + 2 * core * (1 - zm)) + zb) % z_n) * 2 + core
            for y in range(4)
            for zb in range(2)
            for zm in range(2)
        ]
        for first in range(0, z_n, 4)
        for core in range(2)
    ]


def on_device(grads):
    block = grads[0]
    mats, rows_dev, width = block.shape
    dp_n, y_n, core_n = lax.axis_size("dp"), lax.axis_size("y"), lax.axis_size("core")
    far_n, mid_n, near_n = lax.axis_size("zh"), lax.axis_size("zm"), lax.axis_size("zb")
    mats_dp = mats // dp_n
    full_rows = y_n * far_n * mid_n * near_n * core_n * rows_dev
    core = lax.axis_index("core").astype(jnp.int32).reshape(1)
    mid = lax.axis_index("zm")

    slabs = block.reshape(dp_n * y_n * near_n, mid_n, rows_dev, width)
    slabs = lax.all_to_all(slabs, ("dp", "y", "zb"), 0, 0, tiled=True)
    slabs = slabs.reshape(dp_n, y_n * near_n, mid_n, rows_dev, width)

    def summed(which):
        part = lax.dynamic_index_in_dim(slabs, which, 2, keepdims=False)
        return sum(part[i].astype(F32) for i in range(dp_n)).astype(BF16)

    gone, here = lax.optimization_barrier((summed(1 - mid), summed(mid)))
    away = swap_windows(gone)
    mine = jnp.stack([jnp.where(mid == 0, here, away), jnp.where(mid == 0, away, here)], axis=1)
    mine = mine.reshape(mats_dp * rows_dev, width)
    total, sent = half_gram(core, [mine, shift(mine, "core", 1)])
    cut = HALF // 2 // SPARE * SPARE
    totals = [total[:cut], total[cut:]]
    sents = [sent[:cut], sent[cut:]]
    for turn in range(2):
        came = [neighbour(part, "zh", turn) for part in sents]
        totals = [part + other.astype(F32) for part, other in zip(totals, came)]
        sents = [part.astype(BF16) for part in totals]
    others = [shift(part, "core", 1) for part in sents]
    slab = polynomial(core, totals, others, mine, full_rows, mats_dp)
    return slab


def placed(slab, owners, rows_dev, width, full_rows):
    groups = window_groups(lax.axis_size("fsdp"))
    back = lax.all_to_all(slab, "fsdp", 0, 0, axis_index_groups=groups, tiled=True)
    mats_dp = back.shape[0]
    index = lax.axis_index("fsdp")
    owned = lax.dynamic_slice_in_dim(owners, lax.axis_index("dp") * mats_dp, mats_dp)
    hits = owned == index - index % 2
    return place(back, hits, rows_dev, width, full_rows)


def solution(mesh):
    dp_n, fsdp_n = mesh.devices.shape
    shape = (dp_n, 4, fsdp_n // 32, 2, 2, 2)
    grid = Mesh(mesh.devices.reshape(shape), ("dp", *FSDP))

    def run(grads, owners):
        full_rows, width = grads.shape[2:]
        slabs = jax.shard_map(
            on_device,
            mesh=grid,
            in_specs=P("dp", None, FSDP, None),
            out_specs=P(("dp", *FSDP)),
            check_vma=False,
        )(grads)
        return jax.shard_map(
            functools.partial(
                placed, rows_dev=full_rows // fsdp_n, width=width, full_rows=full_rows
            ),
            mesh=mesh,
            in_specs=(P(("dp", "fsdp")), P()),
            out_specs=(P("dp", "fsdp", None), P("dp", "fsdp")),
            check_vma=False,
        )(slabs, owners)

    return run
```
